128 devices in a mesh: orbit: 2 (over core), scene: 16 (over y, x), shard: 4 (over z).
Axes of the slice: x: 4, y: 4, z: 4, core: 2. Of those that a mesh axis runs over, the one named last changes fastest.
Arguments:
- sigma0: bfloat16 [2, 131072, 256], P('orbit', ('scene', 'shard')), may hold values from 0.0001 to 32
- area_tiles: bfloat16 [65536, 256], P(('orbit', 'scene')), may hold values from 0.3984375 to 2.5
- tile_owner: int32 [2, 131072, 1], P('orbit', ('scene', 'shard')), may hold values from 0 to 31; in each aligned block of 2048 rows (0 to 2047, 2048 to 4095, ..., all dimensions but the last counted through in order) at most 128 rows name the same one
- tile_slot: int32 [2, 131072], P('orbit', ('scene', 'shard')), may hold values from 0 to 2047
- trainer_band: int32 [2, 131072, 1], P('orbit', ('scene', 'shard')), may hold values from 0 to 63; in each aligned block of 2048 rows (0 to 2047, 2048 to 4095, ..., all dimensions but the last counted through in order) at most 64 rows name the same one
- seam_offset: int32 [2, 64], P('orbit', ('scene', 'shard')), may hold values from 0 to 63
Outputs:
- patches: float32 [2, 262144, 256], P('orbit', ('scene', 'shard'))
The draws below stay inside these ranges and needn't reach their ends.
Inputs may be any that keep to these rules, and one draw needn't show every extreme that they name: `tile_owner`: within the 2048 rows of one block of one orbit group no owner is named by more than 128 rows, a bound that some block reaches. `trainer_band`: within the 2048 rows of one block of one orbit group no band is named by more than 64 rows, a bound that some block reaches.
All inputs are finite; a program needn't handle non-finite values.
Results may differ from the reference program's by a relative error of at most 0.0025.
Values may be sent and summed in bfloat16 or wider, within the bound.
A program may use at most 64 MiB of HBM per device.

```python
import math
import jax
import jax.numpy as jnp
import numpy as np
from jax import lax

PIX = 256
ROWS_DEV = 2048
TILES_DEV = 2048
ORBITS = 2
OWNERS = 32
TRAINERS = 64
SROWS = 131072
TILES = 65536
CAPT = 128
CAPR = 64


def draw_sigma0(key, part):
    level_key = jax.random.fold_in(key, 11)
    grain_key = jax.random.fold_in(key, 12)
    patch_size = 16
    coarse_rows = SROWS // patch_size + 1
    coarse_cols = PIX // patch_size + 1
    exponent = jax.random.uniform(level_key, (ORBITS, coarse_rows, coarse_cols), jnp.float32, math.log(0.02), math.log(4.0))
    coarse = jnp.exp(exponent)
    line_pos = jnp.arange(SROWS, dtype=jnp.int32) // patch_size
    column_pos = jnp.arange(PIX, dtype=jnp.int32) // patch_size
    backscatter = jnp.take(jnp.take(coarse, line_pos, axis=1), column_pos, axis=2)
    summed = jnp.zeros((ORBITS, SROWS, PIX), jnp.float32)
    for draw_index in range(4):
        uniforms = jax.random.uniform(jax.random.fold_in(grain_key, draw_index), (ORBITS, SROWS, PIX), jnp.float32, 1e-07, 1.0)
        summed = summed - jnp.log(uniforms)
    speckle_gain = jnp.clip(summed / 4.0, 0.005, 8.0)
    return (backscatter * speckle_gain).astype(jnp.bfloat16)


def place_ends(array, rng, least, top_value):
    shape = array.shape
    index_at = [jax.random.randint(jax.random.fold_in(rng, axis), (), 0, shape[axis]) for axis in range(len(shape))]
    array = array.at[tuple(index_at)].set(least)
    longest = shape.index(max(shape))
    index_at[longest] = (index_at[longest] + 1) % shape[longest]
    return array.at[tuple(index_at)].set(top_value)


def shard_levels(stream_key, extent, cuts, smallest, high):
    loudness, own = 1.0, jax.random.fold_in(stream_key, 6)
    for dim, blocks in cuts:
        draws = jnp.exp(jax.random.uniform(jax.random.fold_in(own, dim), (blocks,), jnp.float32, smallest / len(cuts), high / len(cuts)))
        loudness = loudness * jnp.repeat(draws, extent[dim] // blocks).reshape([-1 if axis == dim else 1 for axis in range(len(extent))])
    return loudness


def assign_block(key, own, number, rows, number_of, top, reach, skew):
    sequence = jax.random.permutation(key, number_of)
    crowded, ordinary = shares(number_of, rows * top, reach, skew, True), shares(number_of, rows * top, reach, skew, False)
    places = jnp.arange(number_of)

    def named(lengths, turn):
        used = int((lengths > 0).sum())
        fixed = max(1, used // 4)
        passed = fixed + (places - fixed + turn * (used - fixed)) % max(1, number_of - fixed)
        return jnp.zeros((number_of,), jnp.int32).at[sequence[jnp.where(places < fixed, places, passed)]].set(jnp.asarray(lengths, jnp.int32))

    lengths = jnp.where(number % 4 == 0, named(crowded, number // 4), named(ordinary, number - number // 4 - 1))
    mixed = jax.random.permutation(jax.random.fold_in(own, 3), number_of)
    donor, sink = mixed[0:number_of // 2 * 2:2], mixed[1:number_of // 2 * 2:2]
    room = jnp.minimum(lengths[donor] - 1, reach - lengths[sink]) // 2
    room = jnp.where((donor == sequence[0]) | (sink == sequence[0]) | (lengths[sink] == 0), 0, jnp.maximum(room, 0))
    passed = jax.random.randint(jax.random.fold_in(own, 4), (number_of // 2,), 0, 1 << 20) % (room + 1)
    lengths = lengths.at[donor].add(-passed).at[sink].add(passed)
    labels = jnp.searchsorted(jnp.cumsum(lengths), jnp.arange(rows * top), side="right").astype(jnp.int32)
    table = labels.reshape(top, rows).T
    table = table[jax.random.permutation(jax.random.fold_in(own, 1), rows)]
    turn = jax.random.randint(jax.random.fold_in(own, 2), (rows, 1), 0, top)
    return jnp.take_along_axis(table, (jnp.arange(top)[None, :] + turn) % top, axis=1)


def shares(count, total, limit, lean, full):
    loads = [(1 << 20) // math.isqrt(standing ** lean) + 1 for standing in range(1, count + 1)]
    largest = limit if full else min(limit, max(-(-total // count), total * loads[0] // sum(loads)))
    least = 1 if total - largest >= count - 1 else 0
    given, rest = [largest] + [least] * (count - 1), total - largest - least * (count - 1)
    while rest > 0:
        candidates = [i for i in range(1, count) if given[i] < largest] or [i for i in range(1, count) if given[i] < limit]
        whole, left = sum([loads[i] for i in candidates]), rest
        for i in candidates:
            extra = min(limit - given[i], max(1, left * loads[i] // whole), rest)
            given[i] = given[i] + extra
            rest = rest - extra
    return np.array(given)


def setup_inputs(seed: int = 0) -> dict:
    splits = jax.random.split(jax.random.key(seed), 7)
    sigma0 = draw_sigma0(jax.random.fold_in(splits[6], 71), 0)
    area_tiles = jnp.clip(jnp.exp(math.log(2.5) - 1.8364954 * jax.random.uniform(splits[1], (TILES, PIX), jnp.float32) ** shard_levels(splits[1], (TILES, PIX), ((0, 32),), -0.2, 0.2)), 0.3984375, 2.5).astype(jnp.bfloat16)
    tile_owner_keys = jax.random.split(jax.random.fold_in(splits[2], 1), ORBITS * SROWS // ROWS_DEV)
    tile_owner_turns = jax.random.permutation(jax.random.fold_in(splits[2], 3), ORBITS * SROWS // ROWS_DEV)
    tile_owner = jax.vmap(lambda own, number: assign_block(jax.random.fold_in(splits[2], 2), own, number, ROWS_DEV, OWNERS, 1, CAPT, 2))(tile_owner_keys, tile_owner_turns).reshape((ORBITS, SROWS, 1))
    tile_slot = place_ends(jax.random.randint(splits[3], (ORBITS, SROWS), 0, TILES_DEV), jax.random.fold_in(splits[3], 1), 0, TILES_DEV - 1).astype(jnp.int32)
    trainer_band_keys = jax.random.split(jax.random.fold_in(splits[4], 1), ORBITS * SROWS // ROWS_DEV)
    trainer_band_turns = jax.random.permutation(jax.random.fold_in(splits[4], 3), ORBITS * SROWS // ROWS_DEV)
    trainer_band = jax.vmap(lambda own, number: assign_block(jax.random.fold_in(splits[4], 2), own, number, ROWS_DEV, TRAINERS, 1, CAPR, 2))(trainer_band_keys, trainer_band_turns).reshape((ORBITS, SROWS, 1))
    seam_offset = place_ends(jax.random.randint(splits[5], (ORBITS, TRAINERS), 0, TRAINERS), jax.random.fold_in(splits[5], 1), 0, TRAINERS - 1).astype(jnp.int32)
    return {"sigma0": sigma0, "area_tiles": area_tiles, "tile_owner": tile_owner, "tile_slot": tile_slot, "trainer_band": trainer_band, "seam_offset": seam_offset}


NOISE = 0.25


def window_sum(padded, count_rows, pixels):
    vertical = padded[0:count_rows]
    for offset in range(1, 7):
        vertical = vertical + padded[offset:offset + count_rows]
    widened = jnp.pad(vertical, ((0, 0), (3, 3)))
    window = widened[:, 0:pixels]
    for offset in range(1, 7):
        window = window + widened[:, offset:offset + pixels]
    return window


def lee_filter(intensity, first_row, all_rows):
    count_rows = intensity.shape[0] - 6
    pixels = intensity.shape[1]
    center = intensity[3:3 + count_rows]
    first_sum = window_sum(intensity, count_rows, pixels)
    second = window_sum(intensity * intensity, count_rows, pixels)
    line_idx = first_row + jnp.arange(count_rows, dtype=jnp.int32)
    row_span = jnp.minimum(line_idx + 3, all_rows - 1) - jnp.maximum(line_idx - 3, 0) + 1
    column = jnp.arange(pixels, dtype=jnp.int32)
    col_span = jnp.minimum(column + 3, pixels - 1) - jnp.maximum(column - 3, 0) + 1
    counts = (row_span[:, None] * col_span[None, :]).astype(jnp.float32)
    local_mean = first_sum / counts
    variance = second / counts - local_mean * local_mean
    speckle = NOISE * local_mean * local_mean
    mixing = jnp.maximum(variance - speckle, 0.0) / (variance + speckle)
    return local_mean + mixing * (center - local_mean)


def reference(sigma0, area_tiles, tile_owner, tile_slot, trainer_band, seam_offset):
    all_rows = sigma0.shape[1]
    pixels = sigma0.shape[2]

    def one_orbit(orbit_image):
        intensity = jnp.pad(orbit_image.astype(jnp.float32), ((3, 3), (0, 0)))
        return lee_filter(intensity, 0, all_rows)

    filtered = lax.map(one_orbit, sigma0)
    tile_id = (tile_owner[:, :, 0] * TILES_DEV + tile_slot).astype(jnp.int32)
    weight = jnp.take(area_tiles, tile_id, axis=0).astype(jnp.float32)
    flat = (filtered * weight).astype(jnp.bfloat16)
    offsets = jnp.repeat(seam_offset, ROWS_DEV, axis=1)
    trainer = (trainer_band[:, :, 0] + offsets) % TRAINERS
    grouped = trainer.reshape(ORBITS, TRAINERS, ROWS_DEV).astype(jnp.int32)
    onehot = (grouped[..., None] == jnp.arange(TRAINERS, dtype=jnp.int32)).astype(jnp.int32)
    order_out = jnp.sum((jnp.cumsum(onehot, axis=2) - onehot) * onehot, axis=3)
    source = jnp.arange(TRAINERS, dtype=jnp.int32)[None, :, None]
    target = (grouped * (2 * ROWS_DEV) + source * CAPR + order_out).astype(jnp.int32)
    values = jnp.log(flat.astype(jnp.float32)).reshape(ORBITS, TRAINERS * ROWS_DEV, pixels)
    patches = jnp.zeros((ORBITS, TRAINERS * 2 * ROWS_DEV, pixels), jnp.float32)
    orbit_index = jnp.arange(ORBITS, dtype=jnp.int32)[:, None]
    patches = patches.at[orbit_index, target.reshape(ORBITS, TRAINERS * ROWS_DEV)].set(values)
    return patches
```

```python
import jax
import jax.numpy as jnp
from jax import lax
from jax.experimental import pallas as pl
from jax.experimental.pallas import tpu as pltpu
from jax.sharding import PartitionSpec as P

NOISE = 0.25
ROWS = 2048
PIX = 256
OWNERS = 32
CAPT = 128
TRAINERS = 64
CAPR = 64
RG = 4
TG = 8
HALO = 16
LEE = 64
MESH = pl.DeviceIdType.MESH
F32, BF16 = jnp.float32, jnp.bfloat16
PLANE_STRIDE = 11
CUBE_STRIDE = 23


def iota(shape, dim):
    return lax.broadcasted_iota(jnp.int32, shape, dim).astype(F32)


def dot(a, b):
    return jnp.dot(a, b, preferred_element_type=F32)


def mask(hit):
    return jnp.where(hit, 1.0, 0.0).astype(BF16)


def body(
    sigma, area, owner, slot, band, seam, out,
    sum1, sum2, filtered, weight, flat, source, source_row, target_row,
    ask_out, ask_in, rep_out, rep_in, put_out, put_in, halo_in,
    halo_send, halo_recv, ask_send, ask_recv, rep_send, rep_recv, put_send, put_recv,
):
    orbit, scene, shard = (lax.axis_index(name) for name in ("orbit", "scene", "shard"))
    y, x = scene // 4, scene % 4
    block = scene * 4 + shard

    def plane(k, sign):
        step = (k * PLANE_STRIDE) % OWNERS
        dy, dx = sign * (step // 8) + 4, sign * ((step // 2) % 4) + 4
        return ((orbit + step % 2) % 2, ((y + dy) % 4) * 4 + (x + dx) % 4, shard)

    def cube(k, sign):
        step = (k * CUBE_STRIDE) % TRAINERS
        dy, dx, dz = (sign * d + 4 for d in (step // 16, (step // 4) % 4, step % 4))
        return (orbit, ((y + dy) % 4) * 4 + (x + dx) % 4, (shard + dz) % 4)

    def owner_of(device):
        return device[0] * 16 + device[1]

    def trainer_of(device):
        return device[1] * 4 + device[2]

    barrier = pltpu.get_barrier_semaphore()

    def greet_other(k, carry):
        pl.semaphore_signal(barrier, inc=1, device_id=((orbit + 1) % 2, k, shard), device_id_type=MESH)
        return carry

    def greet_own(k, carry):
        pl.semaphore_signal(barrier, inc=1, device_id=cube(k, 1), device_id_type=MESH)
        return carry

    lax.fori_loop(0, 16, greet_other, 0)
    lax.fori_loop(1, TRAINERS, greet_own, 0)

    upper = mask(iota((256, 256), 0) < iota((256, 256), 1))
    seen = jnp.zeros((OWNERS + TRAINERS, 1), F32)
    wanted = jnp.zeros((2 * OWNERS, CAPT), F32)
    for part in range(ROWS // 256):
        lanes = pl.ds(part * 256, 256)
        own = owner[:, lanes].astype(F32)
        trainer = ((band[:, lanes] + seam[...]) & (TRAINERS - 1)).astype(F32)
        own_hot = jnp.where(iota((OWNERS, 256), 0) == own, 1.0, 0.0)
        trainer_hot = jnp.where(iota((TRAINERS, 256), 0) == trainer, 1.0, 0.0)
        hot = jnp.concatenate([own_hot, trainer_hot], axis=0)
        before = (dot(hot.astype(BF16), upper) + seen) * hot
        seen = seen + jnp.sum(hot, axis=1, keepdims=True)
        order_in = jnp.sum(before[:OWNERS], axis=0, keepdims=True)
        order_out = jnp.sum(before[OWNERS:], axis=0, keepdims=True)
        source_row[:, lanes] = own * CAPT + order_in
        target_row[:, lanes] = trainer * CAPR + order_out
        place = slot[:, lanes]
        high, low = (place >> 8).astype(F32), (place & 255).astype(F32)
        parts = jnp.concatenate([own_hot * high, own_hot * low], axis=0).astype(BF16)
        wanted = wanted + lax.dot_general(
            parts, mask(iota((CAPT, 256), 0) == order_in),
            (((1,), (1,)), ((), ())), preferred_element_type=F32,
        )
    positions = (wanted[:OWNERS] * 256.0 + wanted[OWNERS:]).astype(jnp.int32)
    for index in range(OWNERS):
        ask_out[index] = positions[index : index + 1, :]

    pl.semaphore_wait(barrier, 16 + TRAINERS - 1)

    pltpu.make_async_copy(ask_out.at[owner_of((orbit, scene))], ask_in.at[0], ask_recv.at[0]).start()

    def send_ask(k, carry):
        peer = plane(k, 1)
        pltpu.make_async_remote_copy(
            ask_out.at[owner_of(peer)], ask_in.at[k], ask_send, ask_recv.at[k // RG],
            device_id=peer, device_id_type=MESH,
        ).start()
        return carry

    lax.fori_loop(1, OWNERS, send_ask, 0)

    def halo_copy(side):
        peer = block + 1 - 2 * side
        rows = pl.ds((1 - side) * (ROWS - HALO), HALO)
        return pltpu.make_async_remote_copy(
            sigma.at[rows], halo_in.at[side], halo_send.at[side], halo_recv.at[side],
            device_id=(orbit, peer // 4, peer % 4), device_id_type=MESH,
        )

    has_side = (block > 0, block < TRAINERS - 1)
    for side in range(2):

        @pl.when(has_side[1 - side])
        def _():
            halo_copy(side).start()

        @pl.when(jnp.logical_not(has_side[side]))
        def _():
            halo_in[side] = jnp.zeros((HALO, PIX), BF16)

    near = mask(jnp.abs(iota((PIX, PIX), 0) - iota((PIX, PIX), 1)) < 4.0)

    def row_sums(cells, rows):
        wide = cells.astype(F32)
        square = wide * wide
        high = square.astype(BF16)
        low = (square - high.astype(F32)).astype(BF16)
        sum1[rows] = dot(cells, near)
        sum2[rows] = dot(high, near) + dot(low, near)

    def sums_step(part, carry):
        row_sums(sigma[pl.ds(pl.multiple_of(part * 256, 256), 256)], pl.ds(pl.multiple_of(part * 256 + HALO, HALO), 256))
        return carry

    lax.fori_loop(0, ROWS // 256, sums_step, 0)

    for part in range(ROWS // 128):
        row = source_row[:, pl.ds(part * 128, 128)]
        source[pl.ds(part * 128, 128)] = jnp.transpose(jnp.broadcast_to(row, (128, 128)))

    def gather_step(step, carry):
        group = pl.ds(step * RG, RG)
        pltpu.make_async_copy(ask_in.at[group], ask_in.at[group], ask_recv.at[step]).wait()
        columns = [
            jnp.transpose(jnp.broadcast_to(ask_in[step * RG + j].astype(F32), (CAPT, CAPT)))
            for j in range(RG)
        ]
        column = jnp.concatenate(columns, axis=0)
        lane = iota((RG * CAPT, 128), 1)
        picker = jnp.concatenate([mask(column == lane + 128.0 * c) for c in range(ROWS // 128)], axis=1)
        rep_out[group] = dot(picker, area[...]).astype(BF16).reshape(RG, CAPT, PIX)
        for j in range(RG):
            k = step * RG + j

            @pl.when(k == 0)
            def _():
                pltpu.make_async_copy(rep_out.at[k], rep_in.at[k], rep_recv.at[step]).start()

            @pl.when(k > 0)
            def _():
                pltpu.make_async_remote_copy(
                    rep_out.at[k], rep_in.at[k], rep_send, rep_recv.at[step],
                    device_id=plane(k, -1), device_id_type=MESH,
                ).start()

        return carry

    lax.fori_loop(0, OWNERS // RG, gather_step, 0)

    for side in range(2):

        @pl.when(has_side[side])
        def _():
            halo_copy(side).wait_recv()

        row_sums(halo_in[side], pl.ds(side * (ROWS + HALO), HALO))

    pixel = iota((LEE, PIX), 1)
    col_span = jnp.minimum(pixel + 3.0, PIX - 1.0) - jnp.maximum(pixel - 3.0, 0.0) + 1.0
    line = iota((LEE, PIX), 0)

    def seven(cells):
        rows = cells.shape[0]
        two = cells + pltpu.roll(cells, rows - 1, 0)
        four = two + pltpu.roll(two, rows - 2, 0)
        total = four + pltpu.roll(two, rows - 4, 0) + pltpu.roll(cells, rows - 6, 0)
        return pltpu.roll(total, rows - 5, 0)[:LEE]

    def lee_step(part, carry):
        start = pl.multiple_of(part * LEE, LEE)
        slab = pl.ds(pl.multiple_of(start + 8, 8), LEE + 16)
        at = line + (block * ROWS + start).astype(F32)
        row_span = jnp.minimum(at + 3.0, TRAINERS * ROWS - 1.0) - jnp.maximum(at - 3.0, 0.0) + 1.0
        share = 1.0 / (row_span * col_span)
        center = sigma[pl.ds(start, LEE)].astype(F32)
        mean = seven(sum1[slab]) * share
        power = mean * mean
        variance = seven(sum2[slab]) * share - power
        speckle = NOISE * power
        mixing = jnp.maximum(variance - speckle, 0.0) / (variance + speckle)
        filtered[pl.ds(start, LEE)] = mean + mixing * (center - mean)
        return carry

    lax.fori_loop(0, ROWS // LEE, lee_step, 0)

    def pick_step(step, carry):
        group = pl.ds(step * RG, RG)
        pltpu.make_async_copy(rep_in.at[group], rep_in.at[group], rep_recv.at[step]).wait()
        table = rep_in[group].reshape(RG * CAPT, PIX)
        firsts = [(owner_of(plane(step * RG + j, 1)) * CAPT).astype(F32) for j in range(RG)]
        lane = iota((512, CAPT), 1)

        def rows_step(part, inner):
            rows = pl.ds(pl.multiple_of(part * 512, 512), 512)
            column = source[rows]
            picker = jnp.concatenate([mask(column == lane + first) for first in firsts], axis=1)
            picked = dot(picker, table)
            weight[rows] = jnp.where(step > 0, weight[rows] + picked, picked)
            return inner

        return lax.fori_loop(0, ROWS // 512, rows_step, carry)

    weight[...] = jnp.zeros((ROWS, PIX), F32)
    lax.fori_loop(0, OWNERS // RG, pick_step, 0)
    flat[...] = (filtered[...] * weight[...]).astype(BF16)

    def place_step(step, carry):
        group = pl.ds(step * TG, TG)
        row = target_row[...]
        line = iota((CAPR, ROWS), 0)
        pickers = []
        for j in range(TG):
            first = (trainer_of(cube(step * TG + j, 1)) * CAPR).astype(F32)
            pickers.append(mask(line == row - first))
        placed = dot(jnp.concatenate(pickers, axis=0), flat[...])
        put_out[group] = placed.astype(BF16).reshape(TG, CAPR, PIX)
        for j in range(TG):
            k = step * TG + j

            @pl.when(k == 0)
            def _():
                pltpu.make_async_copy(put_out.at[k], put_in.at[k], put_recv.at[step]).start()

            @pl.when(k > 0)
            def _():
                pltpu.make_async_remote_copy(
                    put_out.at[k], put_in.at[k], put_send, put_recv.at[step],
                    device_id=cube(k, 1), device_id_type=MESH,
                ).start()

        return carry

    lax.fori_loop(0, TRAINERS // TG, place_step, 0)

    def log_step(step, carry):
        group = pl.ds(step * TG, TG)
        pltpu.make_async_copy(put_in.at[group], put_in.at[group], put_recv.at[step]).wait()

        def one(j, inner):
            k = step * TG + j
            values = put_in[k].astype(F32)
            filled = values > 0.0
            logs = jnp.where(filled, jnp.log(jnp.where(filled, values, 1.0)), 0.0)
            first = pl.multiple_of(trainer_of(cube(k, -1)) * CAPR, CAPR)
            out[pl.ds(first, CAPR)] = logs
            return inner

        return lax.fori_loop(0, TG, one, carry)

    lax.fori_loop(0, TRAINERS // TG, log_step, 0)

    for buffer, sem, count in (
        (ask_out, ask_send, OWNERS - 1),
        (rep_out, rep_send, OWNERS - 1),
        (put_out, put_send, TRAINERS - 1),
    ):
        part = buffer.at[pl.ds(1, count)]
        pltpu.make_async_copy(part, part, sem).wait()
    for side in range(2):

        @pl.when(has_side[1 - side])
        def _():
            halo_copy(side).wait_send()


def per_device(sigma0, area_tiles, tile_owner, tile_slot, trainer_band, seam_offset):
    vmem = pl.BlockSpec(memory_space=pltpu.VMEM)
    dma = pltpu.SemaphoreType.DMA
    patches = pl.pallas_call(
        body,
        out_shape=jax.ShapeDtypeStruct((TRAINERS * CAPR, PIX), F32),
        in_specs=[vmem] * 6,
        out_specs=vmem,
        scratch_shapes=[
            pltpu.VMEM((ROWS + 2 * HALO, PIX), F32),
            pltpu.VMEM((ROWS + 2 * HALO, PIX), F32),
            pltpu.VMEM((ROWS, PIX), F32),
            pltpu.VMEM((ROWS, PIX), F32),
            pltpu.VMEM((ROWS, PIX), BF16),
            pltpu.VMEM((ROWS, 128), F32),
            pltpu.VMEM((1, ROWS), F32),
            pltpu.VMEM((1, ROWS), F32),
            pltpu.VMEM((OWNERS, 1, CAPT), jnp.int32),
            pltpu.VMEM((OWNERS, 1, CAPT), jnp.int32),
            pltpu.VMEM((OWNERS, CAPT, PIX), BF16),
            pltpu.VMEM((OWNERS, CAPT, PIX), BF16),
            pltpu.VMEM((TRAINERS, CAPR, PIX), BF16),
            pltpu.VMEM((TRAINERS, CAPR, PIX), BF16),
            pltpu.VMEM((2, HALO, PIX), BF16),
            dma((2,)),
            dma((2,)),
            dma(()),
            dma((OWNERS // RG,)),
            dma(()),
            dma((OWNERS // RG,)),
            dma(()),
            dma((TRAINERS // TG,)),
        ],
        compiler_params=pltpu.CompilerParams(
            collective_id=0, has_side_effects=True, vmem_limit_bytes=50 << 20
        ),
        cost_estimate=pl.CostEstimate(flops=16 << 30, bytes_accessed=8 << 20, transcendentals=1 << 20),
    )(
        sigma0[0],
        area_tiles,
        tile_owner.reshape(1, ROWS),
        tile_slot,
        trainer_band.reshape(1, ROWS),
        seam_offset,
    )
    return patches[None]


def solution(mesh):
    return jax.shard_map(
        per_device,
        mesh=mesh,
        in_specs=(
            P("orbit", ("scene", "shard"), None),
            P(("orbit", "scene"), None),
            P("orbit", ("scene", "shard"), None),
            P("orbit", ("scene", "shard")),
            P("orbit", ("scene", "shard"), None),
            P("orbit", ("scene", "shard")),
        ),
        out_specs=P("orbit", ("scene", "shard"), None),
        check_vma=False,
    )
```

```python
import jax
import jax.numpy as jnp
from jax import lax
from jax.experimental import pallas as pl
from jax.experimental.pallas import tpu as pltpu
from jax.sharding import PartitionSpec as P

NOISE = 0.25
ROWS = 2048
PIX = 256
OWNERS = 32
CAPT = 128
TRAINERS = 64
CAPR = 64
RG = 4
TG = 8
HALO = 16
LEE = 64
MESH = pl.DeviceIdType.MESH
F32, BF16 = jnp.float32, jnp.bfloat16
PLANE_STRIDE = 11
CUBE_STRIDE = 23


def iota(shape, dim):
    return lax.broadcasted_iota(jnp.int32, shape, dim).astype(F32)


def dot(a, b):
    return jnp.dot(a, b, preferred_element_type=F32)


def mask(hit):
    return jnp.where(hit, 1.0, 0.0).astype(BF16)


def body(
    sigma_hbm, area_hbm, owner_hbm, slot_hbm, band_hbm, seam, put_in,
    sigma, area, owner, slot, band, loaded, sum1, sum2, filtered, weight, flat, source, source_row, target_row,
    ask_out, ask_in, rep_out, rep_in, put_out, halo_in,
    halo_send, halo_recv, ask_send, ask_recv, rep_send, rep_recv, put_send, put_recv, planes,
):
    orbit, scene, shard = (lax.axis_index(name) for name in ("orbit", "scene", "shard"))
    y, x = scene // 4, scene % 4
    block = scene * 4 + shard

    def plane(k, sign):
        step = (k * PLANE_STRIDE) % OWNERS
        dy, dx = sign * (step // 8) + 4, sign * ((step // 2) % 4) + 4
        return ((orbit + step % 2) % 2, ((y + dy) % 4) * 4 + (x + dx) % 4, shard)

    def cube(k, sign):
        step = (k * CUBE_STRIDE) % TRAINERS
        dy, dx, dz = (sign * d + 4 for d in (step // 16, (step // 4) % 4, step % 4))
        return (orbit, ((y + dy) % 4) * 4 + (x + dx) % 4, (shard + dz) % 4)

    def owner_of(device):
        return device[0] * 16 + device[1]

    def trainer_of(device):
        return device[1] * 4 + device[2]

    loads = [
        pltpu.make_async_copy(*ends, loaded.at[index])
        for index, ends in enumerate(
            ((owner_hbm, owner), (slot_hbm, slot), (band_hbm, band), (sigma_hbm, sigma), (area_hbm, area))
        )
    ]
    for load in loads:
        load.start()

    barrier = pltpu.get_barrier_semaphore()

    def greet(device):
        pl.semaphore_signal(barrier, inc=1, device_id=device, device_id_type=MESH)

    def greet_plane(k, carry):
        greet(plane(k, 1))
        return carry

    lax.fori_loop(1, OWNERS, greet_plane, 0)
    column = [(orbit, scene, (shard + d) % 4) for d in range(1, 4)]
    for device in column:
        greet(device)
    for side in (1, TRAINERS - 1):
        peer = (block + side) % TRAINERS
        greet((orbit, peer // 4, peer % 4))

    for load in loads[:3]:
        load.wait()

    upper = mask(iota((256, 256), 0) < iota((256, 256), 1))
    seen = jnp.zeros((OWNERS + TRAINERS, 1), F32)
    wanted = jnp.zeros((2 * OWNERS, CAPT), F32)
    for part in range(ROWS // 256):
        lanes = pl.ds(part * 256, 256)
        own = owner[:, lanes].astype(F32)
        trainer = ((band[:, lanes] + seam[...]) & (TRAINERS - 1)).astype(F32)
        own_hot = jnp.where(iota((OWNERS, 256), 0) == own, 1.0, 0.0)
        trainer_hot = jnp.where(iota((TRAINERS, 256), 0) == trainer, 1.0, 0.0)
        hot = jnp.concatenate([own_hot, trainer_hot], axis=0)
        before = (dot(hot.astype(BF16), upper) + seen) * hot
        seen = seen + jnp.sum(hot, axis=1, keepdims=True)
        order_in = jnp.sum(before[:OWNERS], axis=0, keepdims=True)
        order_out = jnp.sum(before[OWNERS:], axis=0, keepdims=True)
        source_row[:, lanes] = own * CAPT + order_in
        target_row[:, lanes] = trainer * CAPR + order_out
        place = slot[:, lanes]
        high, low = (place >> 8).astype(F32), (place & 255).astype(F32)
        parts = jnp.concatenate([own_hot * high, own_hot * low], axis=0).astype(BF16)
        wanted = wanted + lax.dot_general(
            parts, mask(iota((CAPT, 256), 0) == order_in),
            (((1,), (1,)), ((), ())), preferred_element_type=F32,
        )
    positions = (wanted[:OWNERS] * 256.0 + wanted[OWNERS:]).astype(jnp.int32)
    for index in range(OWNERS):
        ask_out[index] = positions[index : index + 1, :]

    pl.semaphore_wait(barrier, OWNERS - 1 + 3 + 2)

    pltpu.make_async_copy(ask_out.at[owner_of((orbit, scene))], ask_in.at[0], ask_recv.at[0]).start()

    def send_ask(k, carry):
        peer = plane(k, 1)
        pltpu.make_async_remote_copy(
            ask_out.at[owner_of(peer)], ask_in.at[k], ask_send, ask_recv.at[k // RG],
            device_id=peer, device_id_type=MESH,
        ).start()
        return carry

    lax.fori_loop(1, OWNERS, send_ask, 0)

    def halo_copy(side):
        peer = block + 1 - 2 * side
        rows = pl.ds((1 - side) * (ROWS - HALO), HALO)
        return pltpu.make_async_remote_copy(
            sigma.at[rows], halo_in.at[side], halo_send.at[side], halo_recv.at[side],
            device_id=(orbit, peer // 4, peer % 4), device_id_type=MESH,
        )

    loads[3].wait()
    has_side = (block > 0, block < TRAINERS - 1)
    for side in range(2):

        @pl.when(has_side[1 - side])
        def _():
            halo_copy(side).start()

        @pl.when(jnp.logical_not(has_side[side]))
        def _():
            halo_in[side] = jnp.zeros((HALO, PIX), BF16)

    near = mask(jnp.abs(iota((PIX, PIX), 0) - iota((PIX, PIX), 1)) < 4.0)

    def row_sums(cells, rows):
        wide = cells.astype(F32)
        square = wide * wide
        high = square.astype(BF16)
        low = (square - high.astype(F32)).astype(BF16)
        sum1[rows] = dot(cells, near)
        sum2[rows] = dot(high, near) + dot(low, near)

    def sums_step(part, carry):
        row_sums(sigma[pl.ds(pl.multiple_of(part * 256, 256), 256)], pl.ds(pl.multiple_of(part * 256 + HALO, HALO), 256))
        return carry

    lax.fori_loop(0, ROWS // 256, sums_step, 0)

    for part in range(ROWS // 128):
        row = source_row[:, pl.ds(part * 128, 128)]
        source[pl.ds(part * 128, 128)] = jnp.transpose(jnp.broadcast_to(row, (128, 128)))

    loads[4].wait()

    def gather_step(step, carry):
        group = pl.ds(step * RG, RG)
        pltpu.make_async_copy(ask_in.at[group], ask_in.at[group], ask_recv.at[step]).wait()
        columns = [
            jnp.transpose(jnp.broadcast_to(ask_in[step * RG + j].astype(F32), (CAPT, CAPT)))
            for j in range(RG)
        ]
        column = jnp.concatenate(columns, axis=0)
        lane = iota((RG * CAPT, 128), 1)
        picker = jnp.concatenate([mask(column == lane + 128.0 * c) for c in range(ROWS // 128)], axis=1)
        rep_out[group] = dot(picker, area[...]).astype(BF16).reshape(RG, CAPT, PIX)
        for j in range(RG):
            k = step * RG + j

            @pl.when(k == 0)
            def _():
                pltpu.make_async_copy(rep_out.at[k], rep_in.at[k], rep_recv.at[step]).start()

            @pl.when(k > 0)
            def _():
                pltpu.make_async_remote_copy(
                    rep_out.at[k], rep_in.at[k], rep_send, rep_recv.at[step],
                    device_id=plane(k, -1), device_id_type=MESH,
                ).start()

        return carry

    lax.fori_loop(0, OWNERS // RG, gather_step, 0)

    for device in column:
        pl.semaphore_signal(planes, inc=1, device_id=device, device_id_type=MESH)

    for side in range(2):

        @pl.when(has_side[side])
        def _():
            halo_copy(side).wait_recv()

        row_sums(halo_in[side], pl.ds(side * (ROWS + HALO), HALO))

    pixel = iota((LEE, PIX), 1)
    col_span = jnp.minimum(pixel + 3.0, PIX - 1.0) - jnp.maximum(pixel - 3.0, 0.0) + 1.0
    line = iota((LEE, PIX), 0)

    def seven(cells):
        rows = cells.shape[0]
        two = cells + pltpu.roll(cells, rows - 1, 0)
        four = two + pltpu.roll(two, rows - 2, 0)
        total = four + pltpu.roll(two, rows - 4, 0) + pltpu.roll(cells, rows - 6, 0)
        return pltpu.roll(total, rows - 5, 0)[:LEE]

    def lee_step(part, carry):
        start = pl.multiple_of(part * LEE, LEE)
        slab = pl.ds(pl.multiple_of(start + 8, 8), LEE + 16)
        at = line + (block * ROWS + start).astype(F32)
        row_span = jnp.minimum(at + 3.0, TRAINERS * ROWS - 1.0) - jnp.maximum(at - 3.0, 0.0) + 1.0
        share = 1.0 / (row_span * col_span)
        center = sigma[pl.ds(start, LEE)].astype(F32)
        mean = seven(sum1[slab]) * share
        power = mean * mean
        variance = seven(sum2[slab]) * share - power
        speckle = NOISE * power
        mixing = jnp.maximum(variance - speckle, 0.0) / (variance + speckle)
        filtered[pl.ds(start, LEE)] = mean + mixing * (center - mean)
        return carry

    lax.fori_loop(0, ROWS // LEE, lee_step, 0)

    def pick_step(step, carry):
        group = pl.ds(step * RG, RG)
        pltpu.make_async_copy(rep_in.at[group], rep_in.at[group], rep_recv.at[step]).wait()
        table = rep_in[group].reshape(RG * CAPT, PIX)
        firsts = [(owner_of(plane(step * RG + j, 1)) * CAPT).astype(F32) for j in range(RG)]
        lane = iota((512, CAPT), 1)

        def rows_step(part, inner):
            rows = pl.ds(pl.multiple_of(part * 512, 512), 512)
            column = source[rows]
            picker = jnp.concatenate([mask(column == lane + first) for first in firsts], axis=1)
            picked = dot(picker, table)
            weight[rows] = jnp.where(step > 0, weight[rows] + picked, picked)
            return inner

        return lax.fori_loop(0, ROWS // 512, rows_step, carry)

    weight[...] = jnp.zeros((ROWS, PIX), F32)
    lax.fori_loop(0, OWNERS // RG, pick_step, 0)
    pl.semaphore_wait(planes, 3)
    flat[...] = (filtered[...] * weight[...]).astype(BF16)

    def place_step(step, carry):
        group = pl.ds(step * TG, TG)
        row = target_row[...]
        line = iota((CAPR, ROWS), 0)
        pickers = []
        for j in range(TG):
            first = (trainer_of(cube(step * TG + j, 1)) * CAPR).astype(F32)
            pickers.append(mask(line == row - first))
        placed = dot(jnp.concatenate(pickers, axis=0), flat[...])
        put_out[group] = placed.astype(BF16).reshape(TG, CAPR, PIX)
        for j in range(TG):
            k = step * TG + j

            @pl.when(k == 0)
            def _():
                pltpu.make_async_copy(put_out.at[k], put_in.at[block], put_recv.at[0]).start()

            @pl.when(k > 0)
            def _():
                pltpu.make_async_remote_copy(
                    put_out.at[k], put_in.at[block], put_send, put_recv.at[0],
                    device_id=cube(k, 1), device_id_type=MESH,
                ).start()

        return carry

    lax.fori_loop(0, TRAINERS // TG, place_step, 0)

    pltpu.make_async_copy(put_in, put_in, put_recv.at[0]).wait()

    for buffer, sem, count in (
        (ask_out, ask_send, OWNERS - 1),
        (rep_out, rep_send, OWNERS - 1),
        (put_out, put_send, TRAINERS - 1),
    ):
        part = buffer.at[pl.ds(1, count)]
        pltpu.make_async_copy(part, part, sem).wait()
    for side in range(2):

        @pl.when(has_side[1 - side])
        def _():
            halo_copy(side).wait_send()


def log_body(values, patches, logs, sems):
    copies = []
    for step in range(TRAINERS // TG):
        rows = pl.ds(step * TG * CAPR, TG * CAPR)
        value = values[pl.ds(step * TG, TG)].reshape(TG * CAPR, PIX).astype(F32)
        filled = value > 0.0
        logs[rows] = jnp.where(filled, jnp.log(jnp.where(filled, value, 1.0)), 0.0)
        copies.append(pltpu.make_async_copy(logs.at[rows], patches.at[rows], sems.at[step]))
        copies[-1].start()
    for copy in copies:
        copy.wait()


def per_device(sigma0, area_tiles, tile_owner, tile_slot, trainer_band, seam_offset):
    vmem = pl.BlockSpec(memory_space=pltpu.VMEM)
    dma = pltpu.SemaphoreType.DMA
    hbm = pl.BlockSpec(memory_space=pltpu.HBM)
    arrived = pl.pallas_call(
        body,
        out_shape=jax.ShapeDtypeStruct((TRAINERS, CAPR, PIX), BF16),
        in_specs=[hbm] * 5 + [vmem],
        out_specs=vmem,
        scratch_shapes=[
            pltpu.VMEM((ROWS, PIX), BF16),
            pltpu.VMEM((ROWS, PIX), BF16),
            pltpu.VMEM((1, ROWS), jnp.int32),
            pltpu.VMEM((1, ROWS), jnp.int32),
            pltpu.VMEM((1, ROWS), jnp.int32),
            dma((5,)),
            pltpu.VMEM((ROWS + 2 * HALO, PIX), F32),
            pltpu.VMEM((ROWS + 2 * HALO, PIX), F32),
            pltpu.VMEM((ROWS, PIX), F32),
            pltpu.VMEM((ROWS, PIX), F32),
            pltpu.VMEM((ROWS, PIX), BF16),
            pltpu.VMEM((ROWS, 128), F32),
            pltpu.VMEM((1, ROWS), F32),
            pltpu.VMEM((1, ROWS), F32),
            pltpu.VMEM((OWNERS, 1, CAPT), jnp.int32),
            pltpu.VMEM((OWNERS, 1, CAPT), jnp.int32),
            pltpu.VMEM((OWNERS, CAPT, PIX), BF16),
            pltpu.VMEM((OWNERS, CAPT, PIX), BF16),
            pltpu.VMEM((TRAINERS, CAPR, PIX), BF16),
            pltpu.VMEM((2, HALO, PIX), BF16),
            dma((2,)),
            dma((2,)),
            dma(()),
            dma((OWNERS // RG,)),
            dma(()),
            dma((OWNERS // RG,)),
            dma(()),
            dma((1,)),
            pltpu.SemaphoreType.REGULAR,
        ],
        compiler_params=pltpu.CompilerParams(
            collective_id=0, has_side_effects=True, vmem_limit_bytes=36 << 20
        ),
        cost_estimate=pl.CostEstimate(flops=16 << 30, bytes_accessed=8 << 20, transcendentals=1 << 20),
    )(
        *(
            pltpu.with_memory_space_constraint(array, pltpu.HBM)
            for array in (
                sigma0[0],
                area_tiles,
                tile_owner.reshape(1, ROWS),
                tile_slot,
                trainer_band.reshape(1, ROWS),
            )
        ),
        seam_offset,
    )
    patches = pl.pallas_call(
        log_body,
        out_shape=jax.ShapeDtypeStruct((TRAINERS * CAPR, PIX), F32),
        in_specs=[vmem],
        out_specs=hbm,
        scratch_shapes=[pltpu.VMEM((TRAINERS * CAPR, PIX), F32), dma((TRAINERS // TG,))],
        compiler_params=pltpu.CompilerParams(vmem_limit_bytes=16 << 20),
    )(arrived)
    return patches[None]


def solution(mesh):
    return jax.shard_map(
        per_device,
        mesh=mesh,
        in_specs=(
            P("orbit", ("scene", "shard"), None),
            P(("orbit", "scene"), None),
            P("orbit", ("scene", "shard"), None),
            P("orbit", ("scene", "shard")),
            P("orbit", ("scene", "shard"), None),
            P("orbit", ("scene", "shard")),
        ),
        out_specs=P("orbit", ("scene", "shard"), None),
        check_vma=False,
    )
```

```python
import functools

import jax
import jax.numpy as jnp
from jax import lax
from jax.experimental import pallas as pl
from jax.experimental.pallas import tpu as pltpu
from jax.sharding import PartitionSpec as P

NOISE = 0.25
ROWS = 2048
PIX = 256
OWNERS = 32
CAPT = 128
TRAINERS = 64
CAPR = 64
RG = 4
PG = (8, 4)
TG = (16, 8)
LOG = 8
HALO = 16
HALF = PIX // 2
LEE = 64
MESH = pl.DeviceIdType.MESH
F32, BF16 = jnp.float32, jnp.bfloat16
PLANE_STRIDE = 27
CUBE_STRIDE = 23


def iota(shape, dim):
    return lax.broadcasted_iota(jnp.int32, shape, dim).astype(F32)


def dot(a, b):
    return jnp.dot(a, b, preferred_element_type=F32)


def rem(a, b):
    return lax.rem(a, jnp.int32(b))


def div(a, b):
    return lax.div(a, jnp.int32(b))


def mask(hit):
    return jnp.where(hit, 1.0, 0.0).astype(BF16)


def body(
    sigma_hbm, area_hbm, owner_hbm, slot_hbm, band_hbm, seam, put_in,
    sigma, area, owner, slot, band, loaded, sum1, sum2, filtered, weight, flat, source, source_row, target_row,
    ask_out, ask_in, rep_out, rep_in, put_out, halo_in,
    halo_send, halo_recv, ask_send, ask_recv, rep_send, rep_recv, put_send, put_recv, planes,
):
    orbit, scene, shard = (lax.axis_index(name) for name in ("orbit", "scene", "shard"))
    y, x = div(scene, 4), rem(scene, 4)
    block = scene * 4 + shard

    def plane(k, sign):
        step = rem(k * PLANE_STRIDE, OWNERS)
        dy, dx = sign * div(step, 8) + 4, sign * rem(div(step, 2), 4) + 4
        return (rem(orbit + rem(step, 2), 2), rem(y + dy, 4) * 4 + rem(x + dx, 4), shard)

    def cube(k, sign):
        step = rem(k * CUBE_STRIDE, TRAINERS)
        dy, dx, dz = (sign * d + 4 for d in (div(step, 16), rem(div(step, 4), 4), rem(step, 4)))
        return (orbit, rem(y + dy, 4) * 4 + rem(x + dx, 4), rem(shard + dz, 4))

    def owner_of(device):
        return device[0] * 16 + device[1]

    def trainer_of(device):
        return device[1] * 4 + device[2]

    loads = [
        pltpu.make_async_copy(*ends, loaded.at[index])
        for index, ends in enumerate(
            ((owner_hbm, owner), (slot_hbm, slot), (band_hbm, band), (sigma_hbm, sigma), (area_hbm, area))
        )
    ]
    for load in loads:
        load.start()

    barrier = pltpu.get_barrier_semaphore()

    def greet(device):
        pl.semaphore_signal(barrier, inc=1, device_id=device, device_id_type=MESH)

    def greet_plane(k, carry):
        greet(plane(k, 1))
        return carry

    lax.fori_loop(1, OWNERS, greet_plane, 0)
    column = [(orbit, scene, rem(shard + d, 4)) for d in range(1, 4)]
    for device in column:
        greet(device)
    for side in (1, TRAINERS - 1):
        peer = rem(block + side, TRAINERS)
        greet((orbit, div(peer, 4), rem(peer, 4)))

    for load in loads[:3]:
        load.wait()

    upper = mask(iota((256, 256), 0) < iota((256, 256), 1))
    seen = jnp.zeros((OWNERS + TRAINERS, 1), F32)
    wanted = jnp.zeros((2 * OWNERS, CAPT), F32)
    for part in range(ROWS // 256):
        lanes = pl.ds(part * 256, 256)
        own = owner[:, lanes].astype(F32)
        trainer = ((band[:, lanes] + seam[...]) & (TRAINERS - 1)).astype(F32)
        own_hot = jnp.where(iota((OWNERS, 256), 0) == own, 1.0, 0.0)
        trainer_hot = jnp.where(iota((TRAINERS, 256), 0) == trainer, 1.0, 0.0)
        hot = jnp.concatenate([own_hot, trainer_hot], axis=0)
        before = (dot(hot.astype(BF16), upper) + seen) * hot
        seen = seen + jnp.sum(hot, axis=1, keepdims=True)
        order_in = jnp.sum(before[:OWNERS], axis=0, keepdims=True)
        order_out = jnp.sum(before[OWNERS:], axis=0, keepdims=True)
        source_row[:, lanes] = own * CAPT + order_in
        target_row[:, lanes] = trainer * CAPR + order_out
        place = slot[:, lanes]
        high, low = (place >> 8).astype(F32), (place & 255).astype(F32)
        parts = jnp.concatenate([own_hot * high, own_hot * low], axis=0).astype(BF16)
        wanted = wanted + lax.dot_general(
            parts, mask(iota((CAPT, 256), 0) == order_in),
            (((1,), (1,)), ((), ())), preferred_element_type=F32,
        )
    positions = (wanted[:OWNERS] * 256.0 + wanted[OWNERS:]).astype(jnp.int32)
    for index in range(OWNERS):
        ask_out[index] = positions[index : index + 1, :]

    loads[3].wait()

    near = mask(jnp.abs(iota((PIX, PIX), 0) - iota((PIX, PIX), 1)) < 4.0)

    def row_sums(cells, rows):
        wide = cells.astype(F32)
        square = wide * wide
        high = square.astype(BF16)
        low = (square - high.astype(F32)).astype(BF16)
        sum1[rows] = dot(cells, near)
        sum2[rows] = dot(high, near) + dot(low, near)

    def sums_step(part, carry):
        row_sums(sigma[pl.ds(pl.multiple_of(part * 256, 256), 256)], pl.ds(pl.multiple_of(part * 256 + HALO, HALO), 256))
        return carry

    lax.fori_loop(0, ROWS // 256, sums_step, 0)

    for part in range(ROWS // 128):
        row = source_row[:, pl.ds(part * 128, 128)]
        source[pl.ds(part * 128, 128)] = jnp.transpose(jnp.broadcast_to(row, (128, 128)))

    pl.semaphore_wait(barrier, OWNERS - 1 + 3 + 2)

    pltpu.make_async_copy(ask_out.at[owner_of((orbit, scene))], ask_in.at[0], ask_recv.at[0]).start()

    def send_ask(k, carry):
        peer = plane(k, 1)
        pltpu.make_async_remote_copy(
            ask_out.at[owner_of(peer)], ask_in.at[k], ask_send, ask_recv.at[div(k, RG)],
            device_id=peer, device_id_type=MESH,
        ).start()
        return carry

    lax.fori_loop(1, OWNERS, send_ask, 0)

    def halo_copy(side):
        peer = block + 1 - 2 * side
        rows = pl.ds((1 - side) * (ROWS - HALO), HALO)
        return pltpu.make_async_remote_copy(
            sigma.at[rows], halo_in.at[side], halo_send.at[side], halo_recv.at[side],
            device_id=(orbit, div(peer, 4), rem(peer, 4)), device_id_type=MESH,
        )

    has_side = (block > 0, block < TRAINERS - 1)
    for side in range(2):

        @pl.when(has_side[1 - side])
        def _():
            halo_copy(side).start()

        @pl.when(jnp.logical_not(has_side[side]))
        def _():
            halo_in[side] = jnp.zeros((HALO, PIX), BF16)

    loads[4].wait()

    def reply(half, k):
        step = div(k, PG[half])

        @pl.when(k == 0)
        def _():
            pltpu.make_async_copy(rep_out.at[half, k], rep_in.at[half, k], rep_recv.at[half, step]).start()

        @pl.when(k > 0)
        def _():
            pltpu.make_async_remote_copy(
                rep_out.at[half, k], rep_in.at[half, k], rep_send.at[half], rep_recv.at[half, step],
                device_id=plane(k, -1), device_id_type=MESH,
            ).start()

    def gather_step(step, carry):
        group = pl.ds(step * RG, RG)
        pltpu.make_async_copy(ask_in.at[group], ask_in.at[group], ask_recv.at[step]).wait()
        columns = [
            jnp.transpose(jnp.broadcast_to(ask_in[step * RG + j].astype(F32), (CAPT, CAPT)))
            for j in range(RG)
        ]
        column = jnp.concatenate(columns, axis=0)
        lane = iota((RG * CAPT, 128), 1)
        picker = jnp.concatenate([mask(column == lane + 128.0 * c) for c in range(ROWS // 128)], axis=1)
        picked = dot(picker, area[...]).astype(BF16)
        for half in range(2):
            rep_out[half, group] = picked[:, half * HALF : (half + 1) * HALF].reshape(RG, CAPT, HALF)
        for j in range(RG):
            reply(0, step * RG + j)
        return carry

    lax.fori_loop(0, OWNERS // RG, gather_step, 0)

    def reply_rest(k, carry):
        reply(1, k)
        return carry

    lax.fori_loop(0, OWNERS, reply_rest, 0)

    for device in column:
        pl.semaphore_signal(planes, inc=1, device_id=device, device_id_type=MESH)

    for side in range(2):

        @pl.when(has_side[side])
        def _():
            halo_copy(side).wait_recv()

        row_sums(halo_in[side], pl.ds(side * (ROWS + HALO), HALO))

    pixel = iota((LEE, PIX), 1)
    col_span = jnp.minimum(pixel + 3.0, PIX - 1.0) - jnp.maximum(pixel - 3.0, 0.0) + 1.0
    line = iota((LEE, PIX), 0)

    def seven(cells):
        rows = cells.shape[0]
        two = cells + pltpu.roll(cells, rows - 1, 0)
        four = two + pltpu.roll(two, rows - 2, 0)
        total = four + pltpu.roll(two, rows - 4, 0) + pltpu.roll(cells, rows - 6, 0)
        return pltpu.roll(total, rows - 5, 0)[:LEE]

    def lee_step(part, carry):
        start = pl.multiple_of(part * LEE, LEE)
        slab = pl.ds(pl.multiple_of(start + 8, 8), LEE + 16)
        at = line + (block * ROWS + start).astype(F32)
        row_span = jnp.minimum(at + 3.0, TRAINERS * ROWS - 1.0) - jnp.maximum(at - 3.0, 0.0) + 1.0
        share = 1.0 / (row_span * col_span)
        center = sigma[pl.ds(start, LEE)].astype(F32)
        mean = seven(sum1[slab]) * share
        power = mean * mean
        variance = seven(sum2[slab]) * share - power
        speckle = NOISE * power
        mixing = jnp.maximum(variance - speckle, 0.0) / (variance + speckle)
        filtered[pl.ds(start, LEE)] = mean + mixing * (center - mean)
        return carry

    lax.fori_loop(0, ROWS // LEE, lee_step, 0)

    def pick_step(half, step, carry):
        group = pl.ds(step * PG[half], PG[half])
        landed = rep_in.at[half, group]
        pltpu.make_async_copy(landed, landed, rep_recv.at[half, step]).wait()
        table = rep_in[half, group].reshape(PG[half] * CAPT, HALF)
        firsts = [(owner_of(plane(step * PG[half] + j, 1)) * CAPT).astype(F32) for j in range(PG[half])]
        lane = iota((ROWS, CAPT), 1)
        column = source[...]
        picker = jnp.concatenate([mask(column == lane + first) for first in firsts], axis=1)
        weight[...] = weight[...] + dot(picker, table)
        return carry

    def place_step(half, step, carry):
        group = pl.ds(step * TG[half], TG[half])
        row = target_row[...]
        line = iota((CAPR, ROWS), 0)
        pickers = []
        for j in range(TG[half]):
            first = (trainer_of(cube(step * TG[half] + j, 1)) * CAPR).astype(F32)
            pickers.append(mask(line == row - first))
        placed = dot(jnp.concatenate(pickers, axis=0), flat[...])
        put_out[half, group] = placed.astype(BF16).reshape(TG[half], CAPR, HALF)
        for j in range(TG[half]):
            k = step * TG[half] + j

            @pl.when(k == 0)
            def _():
                pltpu.make_async_copy(put_out.at[half, k], put_in.at[half, block], put_recv.at[half]).start()

            @pl.when(k > 0)
            def _():
                pltpu.make_async_remote_copy(
                    put_out.at[half, k], put_in.at[half, block], put_send.at[half], put_recv.at[half],
                    device_id=cube(k, 1), device_id_type=MESH,
                ).start()

        return carry

    for half in range(2):
        weight[...] = jnp.zeros((ROWS, HALF), F32)
        lax.fori_loop(0, OWNERS // PG[half], functools.partial(pick_step, half), 0)
        if half == 0:
            pl.semaphore_wait(planes, 3)
        flat[...] = (filtered[:, half * HALF : (half + 1) * HALF] * weight[...]).astype(BF16)
        lax.fori_loop(0, TRAINERS // TG[half], functools.partial(place_step, half), 0)

    for half in range(2):
        pltpu.make_async_copy(put_in.at[half], put_in.at[half], put_recv.at[half]).wait()

    sent = [(ask_out.at[pl.ds(1, OWNERS - 1)], ask_send)]
    for half in range(2):
        sent.append((rep_out.at[half, pl.ds(1, OWNERS - 1)], rep_send.at[half]))
        sent.append((put_out.at[half, pl.ds(1, TRAINERS - 1)], put_send.at[half]))
    for part, sem in sent:
        pltpu.make_async_copy(part, part, sem).wait()
    for side in range(2):

        @pl.when(has_side[1 - side])
        def _():
            halo_copy(side).wait_send()


def log_body(values, patches, logs, sems):
    copies = []
    for step in range(TRAINERS // LOG):
        rows = pl.ds(step * LOG * CAPR, LOG * CAPR)
        for half in range(2):
            value = values[half, pl.ds(step * LOG, LOG)].reshape(LOG * CAPR, HALF).astype(F32)
            filled = value > 0.0
            logs[rows, half * HALF : (half + 1) * HALF] = jnp.where(
                filled, jnp.log(jnp.where(filled, value, 1.0)), 0.0
            )
        copies.append(pltpu.make_async_copy(logs.at[rows], patches.at[rows], sems.at[step]))
        copies[-1].start()
    for copy in copies:
        copy.wait()


def per_device(sigma0, area_tiles, tile_owner, tile_slot, trainer_band, seam_offset):
    vmem = pl.BlockSpec(memory_space=pltpu.VMEM)
    dma = pltpu.SemaphoreType.DMA
    hbm = pl.BlockSpec(memory_space=pltpu.HBM)
    arrived = pl.pallas_call(
        body,
        out_shape=jax.ShapeDtypeStruct((2, TRAINERS, CAPR, HALF), BF16),
        in_specs=[hbm] * 5 + [vmem],
        out_specs=vmem,
        scratch_shapes=[
            pltpu.VMEM((ROWS, PIX), BF16),
            pltpu.VMEM((ROWS, PIX), BF16),
            pltpu.VMEM((1, ROWS), jnp.int32),
            pltpu.VMEM((1, ROWS), jnp.int32),
            pltpu.VMEM((1, ROWS), jnp.int32),
            dma((5,)),
            pltpu.VMEM((ROWS + 2 * HALO, PIX), F32),
            pltpu.VMEM((ROWS + 2 * HALO, PIX), F32),
            pltpu.VMEM((ROWS, PIX), F32),
            pltpu.VMEM((ROWS, HALF), F32),
            pltpu.VMEM((ROWS, HALF), BF16),
            pltpu.VMEM((ROWS, 128), F32),
            pltpu.VMEM((1, ROWS), F32),
            pltpu.VMEM((1, ROWS), F32),
            pltpu.VMEM((OWNERS, 1, CAPT), jnp.int32),
            pltpu.VMEM((OWNERS, 1, CAPT), jnp.int32),
            pltpu.VMEM((2, OWNERS, CAPT, HALF), BF16),
            pltpu.VMEM((2, OWNERS, CAPT, HALF), BF16),
            pltpu.VMEM((2, TRAINERS, CAPR, HALF), BF16),
            pltpu.VMEM((2, HALO, PIX), BF16),
            dma((2,)),
            dma((2,)),
            dma(()),
            dma((OWNERS // RG,)),
            dma((2,)),
            dma((2, OWNERS // min(PG))),
            dma((2,)),
            dma((2,)),
            pltpu.SemaphoreType.REGULAR,
        ],
        compiler_params=pltpu.CompilerParams(
            collective_id=0, has_side_effects=True, vmem_limit_bytes=36 << 20
        ),
        cost_estimate=pl.CostEstimate(flops=16 << 30, bytes_accessed=8 << 20, transcendentals=1 << 20),
    )(
        *(
            pltpu.with_memory_space_constraint(array, pltpu.HBM)
            for array in (
                sigma0[0],
                area_tiles,
                tile_owner.reshape(1, ROWS),
                tile_slot,
                trainer_band.reshape(1, ROWS),
            )
        ),
        seam_offset,
    )
    patches = pl.pallas_call(
        log_body,
        out_shape=jax.ShapeDtypeStruct((TRAINERS * CAPR, PIX), F32),
        in_specs=[vmem],
        out_specs=hbm,
        scratch_shapes=[pltpu.VMEM((TRAINERS * CAPR, PIX), F32), dma((TRAINERS // LOG,))],
        compiler_params=pltpu.CompilerParams(vmem_limit_bytes=16 << 20),
    )(arrived)
    return patches[None]


def solution(mesh):
    return jax.shard_map(
        per_device,
        mesh=mesh,
        in_specs=(
            P("orbit", ("scene", "shard"), None),
            P(("orbit", "scene"), None),
            P("orbit", ("scene", "shard"), None),
            P("orbit", ("scene", "shard")),
            P("orbit", ("scene", "shard"), None),
            P("orbit", ("scene", "shard")),
        ),
        out_specs=P("orbit", ("scene", "shard"), None),
        check_vma=False,
    )
```

```python
import functools

import jax
import jax.numpy as jnp
from jax import lax
from jax.experimental import pallas as pl
from jax.experimental.pallas import tpu as pltpu
from jax.sharding import PartitionSpec as P

NOISE = 0.25
ROWS = 2048
PIX = 256
OWNERS = 32
CAPT = 128
TRAINERS = 64
CAPR = 64
RG = 4
PG = (8, 4)
TG = (16, 8)
LOG = 4
HALO = 16
HALF = PIX // 2
LEE = 64
MESH = pl.DeviceIdType.MESH
F32, BF16 = jnp.float32, jnp.bfloat16
PLANE_STRIDE = 27
CUBE_STRIDE = 23


def iota(shape, dim):
    return lax.broadcasted_iota(jnp.int32, shape, dim).astype(F32)


def dot(a, b):
    return jnp.dot(a, b, preferred_element_type=F32)


def rem(a, b):
    return lax.rem(a, jnp.int32(b))


def div(a, b):
    return lax.div(a, jnp.int32(b))


def mask(hit):
    return jnp.where(hit, 1.0, 0.0).astype(BF16)


def body(
    sigma_hbm, area_hbm, owner_hbm, slot_hbm, band_hbm, seam, put_in,
    sigma, area, owner, slot, band, loaded, sum1, sum2, filtered, weight, flat, source, source_row, target_row,
    ask_out, ask_in, rep_out, rep_in, put_out, halo_in,
    halo_send, halo_recv, ask_send, ask_recv, rep_send, rep_recv, put_send, put_recv, planes,
):
    orbit, scene, shard = (lax.axis_index(name) for name in ("orbit", "scene", "shard"))
    y, x = div(scene, 4), rem(scene, 4)
    block = scene * 4 + shard

    def plane(k, sign):
        step = rem(k * PLANE_STRIDE, OWNERS)
        dy, dx = sign * div(step, 8) + 4, sign * rem(div(step, 2), 4) + 4
        return (rem(orbit + rem(step, 2), 2), rem(y + dy, 4) * 4 + rem(x + dx, 4), shard)

    def cube(k, sign):
        step = rem(k * CUBE_STRIDE, TRAINERS)
        dy, dx, dz = (sign * d + 4 for d in (div(step, 16), rem(div(step, 4), 4), rem(step, 4)))
        return (orbit, rem(y + dy, 4) * 4 + rem(x + dx, 4), rem(shard + dz, 4))

    def owner_of(device):
        return device[0] * 16 + device[1]

    def trainer_of(device):
        return device[1] * 4 + device[2]

    barrier = pltpu.get_barrier_semaphore()

    def greet(device):
        pl.semaphore_signal(barrier, inc=1, device_id=device, device_id_type=MESH)

    orbits = [rem(orbit + d, 2) for d in range(2)]
    rows_of = [rem(y + d, 4) * 4 for d in range(4)]
    columns_of = [rem(x + d, 4) for d in range(4)]

    def at(offset):
        return (orbits[offset % 2], rows_of[offset // 8] + columns_of[offset // 2 % 4], shard)

    def hops(offset):
        return -sum(min(d, 4 - d) for d in (offset // 8, offset // 2 % 4))

    for offset in sorted(range(1, OWNERS), key=hops):
        greet(at(offset))
    column = [(orbit, scene, rem(shard + d, 4)) for d in range(1, 4)]
    for device in column:
        greet(device)
    for side in (1, TRAINERS - 1):
        peer = rem(block + side, TRAINERS)
        greet((orbit, div(peer, 4), rem(peer, 4)))

    loads = [
        pltpu.make_async_copy(*ends, loaded.at[index])
        for index, ends in enumerate(
            ((owner_hbm, owner), (slot_hbm, slot), (band_hbm, band), (sigma_hbm, sigma), (area_hbm, area))
        )
    ]
    for load in loads:
        load.start()

    for load in loads[:3]:
        load.wait()

    upper = mask(iota((256, 256), 0) < iota((256, 256), 1))
    seen = jnp.zeros((OWNERS + TRAINERS, 1), F32)
    wanted = jnp.zeros((2 * OWNERS, CAPT), F32)
    for part in range(ROWS // 256):
        lanes = pl.ds(part * 256, 256)
        own = owner[:, lanes].astype(F32)
        trainer = ((band[:, lanes] + seam[...]) & (TRAINERS - 1)).astype(F32)
        own_hot = jnp.where(iota((OWNERS, 256), 0) == own, 1.0, 0.0)
        trainer_hot = jnp.where(iota((TRAINERS, 256), 0) == trainer, 1.0, 0.0)
        hot = jnp.concatenate([own_hot, trainer_hot], axis=0)
        before = (dot(hot.astype(BF16), upper) + seen) * hot
        seen = seen + jnp.sum(hot, axis=1, keepdims=True)
        order_in = jnp.sum(before[:OWNERS], axis=0, keepdims=True)
        order_out = jnp.sum(before[OWNERS:], axis=0, keepdims=True)
        source_row[:, lanes] = own * CAPT + order_in
        target_row[:, lanes] = trainer * CAPR + order_out
        place = slot[:, lanes]
        high, low = (place >> 8).astype(F32), (place & 255).astype(F32)
        parts = jnp.concatenate([own_hot * high, own_hot * low], axis=0).astype(BF16)
        wanted = wanted + lax.dot_general(
            parts, mask(iota((CAPT, 256), 0) == order_in),
            (((1,), (1,)), ((), ())), preferred_element_type=F32,
        )
    positions = (wanted[:OWNERS] * 256.0 + wanted[OWNERS:]).astype(jnp.int32)
    for index in range(OWNERS):
        ask_out[index] = positions[index : index + 1, :]

    pl.semaphore_wait(barrier, OWNERS - 1 + 3 + 2)

    pltpu.make_async_copy(ask_out.at[owner_of((orbit, scene))], ask_in.at[0], ask_recv.at[0]).start()

    def send_ask(k, carry):
        peer = plane(k, 1)
        pltpu.make_async_remote_copy(
            ask_out.at[owner_of(peer)], ask_in.at[k], ask_send, ask_recv.at[div(k, RG)],
            device_id=peer, device_id_type=MESH,
        ).start()
        return carry

    lax.fori_loop(1, OWNERS, send_ask, 0)

    def halo_copy(side):
        peer = block + 1 - 2 * side
        rows = pl.ds((1 - side) * (ROWS - HALO), HALO)
        return pltpu.make_async_remote_copy(
            sigma.at[rows], halo_in.at[side], halo_send.at[side], halo_recv.at[side],
            device_id=(orbit, div(peer, 4), rem(peer, 4)), device_id_type=MESH,
        )

    loads[3].wait()
    has_side = (block > 0, block < TRAINERS - 1)
    for side in range(2):

        @pl.when(has_side[1 - side])
        def _():
            halo_copy(side).start()

        @pl.when(jnp.logical_not(has_side[side]))
        def _():
            halo_in[side] = jnp.zeros((HALO, PIX), BF16)

    near = mask(jnp.abs(iota((PIX, PIX), 0) - iota((PIX, PIX), 1)) < 4.0)

    def row_sums(cells, rows):
        wide = cells.astype(F32)
        square = wide * wide
        high = square.astype(BF16)
        low = (square - high.astype(F32)).astype(BF16)
        sum1[rows] = dot(cells, near)
        sum2[rows] = dot(high, near) + dot(low, near)

    def sums_step(part, carry):
        row_sums(sigma[pl.ds(pl.multiple_of(part * 256, 256), 256)], pl.ds(pl.multiple_of(part * 256 + HALO, HALO), 256))
        return carry

    lax.fori_loop(0, ROWS // 256, sums_step, 0)

    loads[4].wait()

    def reply(half, k):
        step = div(k, PG[half])

        @pl.when(k == 0)
        def _():
            pltpu.make_async_copy(rep_out.at[half, k], rep_in.at[half, k], rep_recv.at[half, step]).start()

        @pl.when(k > 0)
        def _():
            pltpu.make_async_remote_copy(
                rep_out.at[half, k], rep_in.at[half, k], rep_send.at[half], rep_recv.at[half, step],
                device_id=plane(k, -1), device_id_type=MESH,
            ).start()

    def gather_step(step, carry):
        group = pl.ds(step * RG, RG)
        pltpu.make_async_copy(ask_in.at[group], ask_in.at[group], ask_recv.at[step]).wait()
        columns = [
            jnp.transpose(jnp.broadcast_to(ask_in[step * RG + j].astype(F32), (CAPT, CAPT)))
            for j in range(RG)
        ]
        column = jnp.concatenate(columns, axis=0)
        lane = iota((RG * CAPT, 128), 1)
        picker = jnp.concatenate([mask(column == lane + 128.0 * c) for c in range(ROWS // 128)], axis=1)
        picked = dot(picker, area[...]).astype(BF16)
        for half in range(2):
            rep_out[half, group] = picked[:, half * HALF : (half + 1) * HALF].reshape(RG, CAPT, HALF)
        for j in range(RG):
            reply(0, step * RG + j)
        return carry

    lax.fori_loop(0, OWNERS // RG, gather_step, 0)

    def reply_rest(k, carry):
        reply(1, k)
        return carry

    lax.fori_loop(0, OWNERS, reply_rest, 0)

    for device in column:
        pl.semaphore_signal(planes, inc=1, device_id=device, device_id_type=MESH)

    for side in range(2):

        @pl.when(has_side[side])
        def _():
            halo_copy(side).wait_recv()

        row_sums(halo_in[side], pl.ds(side * (ROWS + HALO), HALO))

    pixel = iota((LEE, PIX), 1)
    col_span = jnp.minimum(pixel + 3.0, PIX - 1.0) - jnp.maximum(pixel - 3.0, 0.0) + 1.0
    line = iota((LEE, PIX), 0)

    def seven(cells):
        rows = cells.shape[0]
        two = cells + pltpu.roll(cells, rows - 1, 0)
        four = two + pltpu.roll(two, rows - 2, 0)
        total = four + pltpu.roll(two, rows - 4, 0) + pltpu.roll(cells, rows - 6, 0)
        return pltpu.roll(total, rows - 5, 0)[:LEE]

    def lee_step(part, carry):
        start = pl.multiple_of(part * LEE, LEE)
        slab = pl.ds(pl.multiple_of(start + 8, 8), LEE + 16)
        at = line + (block * ROWS + start).astype(F32)
        row_span = jnp.minimum(at + 3.0, TRAINERS * ROWS - 1.0) - jnp.maximum(at - 3.0, 0.0) + 1.0
        share = 1.0 / (row_span * col_span)
        center = sigma[pl.ds(start, LEE)].astype(F32)
        mean = seven(sum1[slab]) * share
        power = mean * mean
        variance = seven(sum2[slab]) * share - power
        speckle = NOISE * power
        mixing = jnp.maximum(variance - speckle, 0.0) / (variance + speckle)
        filtered[pl.ds(start, LEE)] = mean + mixing * (center - mean)
        return carry

    lax.fori_loop(0, ROWS // LEE, lee_step, 0)

    for part in range(ROWS // 128):
        row = source_row[:, pl.ds(part * 128, 128)]
        source[pl.ds(part * 128, 128)] = jnp.transpose(jnp.broadcast_to(row, (128, 128)))


    def pick_step(half, step, carry):
        group = pl.ds(step * PG[half], PG[half])
        landed = rep_in.at[half, group]
        pltpu.make_async_copy(landed, landed, rep_recv.at[half, step]).wait()
        table = rep_in[half, group].reshape(PG[half] * CAPT, HALF)
        firsts = [(owner_of(plane(step * PG[half] + j, 1)) * CAPT).astype(F32) for j in range(PG[half])]
        lane = iota((ROWS, CAPT), 1)
        column = source[...]
        picker = jnp.concatenate([mask(column == lane + first) for first in firsts], axis=1)
        weight[...] = weight[...] + dot(picker, table)
        return carry

    def place_step(half, step, carry):
        group = pl.ds(step * TG[half], TG[half])
        row = target_row[...]
        line = iota((CAPR, ROWS), 0)
        pickers = []
        for j in range(TG[half]):
            first = (trainer_of(cube(step * TG[half] + j, 1)) * CAPR).astype(F32)
            pickers.append(mask(line == row - first))
        placed = dot(jnp.concatenate(pickers, axis=0), flat[...])
        put_out[half, group] = placed.astype(BF16).reshape(TG[half], CAPR, HALF)
        for j in range(TG[half]):
            k = step * TG[half] + j

            @pl.when(k == 0)
            def _():
                pltpu.make_async_copy(put_out.at[half, k], put_in.at[half, block], put_recv.at[half]).start()

            @pl.when(k > 0)
            def _():
                pltpu.make_async_remote_copy(
                    put_out.at[half, k], put_in.at[half, block], put_send.at[half], put_recv.at[half],
                    device_id=cube(k, 1), device_id_type=MESH,
                ).start()

        return carry

    for half in range(2):
        weight[...] = jnp.zeros((ROWS, HALF), F32)
        lax.fori_loop(0, OWNERS // PG[half], functools.partial(pick_step, half), 0)
        if half == 0:
            pl.semaphore_wait(planes, 3)
        flat[...] = (filtered[:, half * HALF : (half + 1) * HALF] * weight[...]).astype(BF16)
        lax.fori_loop(0, TRAINERS // TG[half], functools.partial(place_step, half), 0)

    for half in range(2):
        pltpu.make_async_copy(put_in.at[half], put_in.at[half], put_recv.at[half]).wait()

    sent = [(ask_out.at[pl.ds(1, OWNERS - 1)], ask_send)]
    for half in range(2):
        sent.append((rep_out.at[half, pl.ds(1, OWNERS - 1)], rep_send.at[half]))
        sent.append((put_out.at[half, pl.ds(1, TRAINERS - 1)], put_send.at[half]))
    for part, sem in sent:
        pltpu.make_async_copy(part, part, sem).wait()
    for side in range(2):

        @pl.when(has_side[1 - side])
        def _():
            halo_copy(side).wait_send()


def log_body(values, patches, logs, sems):
    copies = []
    for step in range(TRAINERS // LOG):
        rows = pl.ds(step * LOG * CAPR, LOG * CAPR)
        for half in range(2):
            value = values[half, pl.ds(step * LOG, LOG)].reshape(LOG * CAPR, HALF).astype(F32)
            logs[rows, half * HALF : (half + 1) * HALF] = jnp.where(value > 0.0, jnp.log(value), 0.0)
        copies.append(pltpu.make_async_copy(logs.at[rows], patches.at[rows], sems.at[step]))
        copies[-1].start()
    for copy in copies:
        copy.wait()


def per_device(sigma0, area_tiles, tile_owner, tile_slot, trainer_band, seam_offset):
    vmem = pl.BlockSpec(memory_space=pltpu.VMEM)
    dma = pltpu.SemaphoreType.DMA
    hbm = pl.BlockSpec(memory_space=pltpu.HBM)
    arrived = pl.pallas_call(
        body,
        out_shape=jax.ShapeDtypeStruct((2, TRAINERS, CAPR, HALF), BF16),
        in_specs=[hbm] * 5 + [vmem],
        out_specs=vmem,
        scratch_shapes=[
            pltpu.VMEM((ROWS, PIX), BF16),
            pltpu.VMEM((ROWS, PIX), BF16),
            pltpu.VMEM((1, ROWS), jnp.int32),
            pltpu.VMEM((1, ROWS), jnp.int32),
            pltpu.VMEM((1, ROWS), jnp.int32),
            dma((5,)),
            pltpu.VMEM((ROWS + 2 * HALO, PIX), F32),
            pltpu.VMEM((ROWS + 2 * HALO, PIX), F32),
            pltpu.VMEM((ROWS, PIX), F32),
            pltpu.VMEM((ROWS, HALF), F32),
            pltpu.VMEM((ROWS, HALF), BF16),
            pltpu.VMEM((ROWS, 128), F32),
            pltpu.VMEM((1, ROWS), F32),
            pltpu.VMEM((1, ROWS), F32),
            pltpu.VMEM((OWNERS, 1, CAPT), jnp.int32),
            pltpu.VMEM((OWNERS, 1, CAPT), jnp.int32),
            pltpu.VMEM((2, OWNERS, CAPT, HALF), BF16),
            pltpu.VMEM((2, OWNERS, CAPT, HALF), BF16),
            pltpu.VMEM((2, TRAINERS, CAPR, HALF), BF16),
            pltpu.VMEM((2, HALO, PIX), BF16),
            dma((2,)),
            dma((2,)),
            dma(()),
            dma((OWNERS // RG,)),
            dma((2,)),
            dma((2, OWNERS // min(PG))),
            dma((2,)),
            dma((2,)),
            pltpu.SemaphoreType.REGULAR,
        ],
        compiler_params=pltpu.CompilerParams(
            collective_id=0, has_side_effects=True, vmem_limit_bytes=36 << 20
        ),
        cost_estimate=pl.CostEstimate(flops=16 << 30, bytes_accessed=8 << 20, transcendentals=1 << 20),
    )(
        *(
            pltpu.with_memory_space_constraint(array, pltpu.HBM)
            for array in (
                sigma0[0],
                area_tiles,
                tile_owner.reshape(1, ROWS),
                tile_slot,
                trainer_band.reshape(1, ROWS),
            )
        ),
        seam_offset,
    )
    patches = pl.pallas_call(
        log_body,
        out_shape=jax.ShapeDtypeStruct((TRAINERS * CAPR, PIX), F32),
        in_specs=[vmem],
        out_specs=hbm,
        scratch_shapes=[pltpu.VMEM((TRAINERS * CAPR, PIX), F32), dma((TRAINERS // LOG,))],
        compiler_params=pltpu.CompilerParams(vmem_limit_bytes=16 << 20),
    )(arrived)
    return patches[None]


def solution(mesh):
    return jax.shard_map(
        per_device,
        mesh=mesh,
        in_specs=(
            P("orbit", ("scene", "shard"), None),
            P(("orbit", "scene"), None),
            P("orbit", ("scene", "shard"), None),
            P("orbit", ("scene", "shard")),
            P("orbit", ("scene", "shard"), None),
            P("orbit", ("scene", "shard")),
        ),
        out_specs=P("orbit", ("scene", "shard"), None),
        check_vma=False,
    )
```

```python
import functools

import jax
import jax.numpy as jnp
from jax import lax
from jax.experimental import pallas as pl
from jax.experimental.pallas import tpu as pltpu
from jax.sharding import PartitionSpec as P

NOISE = 0.25
ROWS = 2048
PIX = 256
OWNERS = 32
CAPT = 128
TRAINERS = 64
CAPR = 64
RG = 2
PG = (8, 4)
TG = (16, 4)
LOG = 4
HALO = 16
HALF = PIX // 2
LEE = 64
MESH = pl.DeviceIdType.MESH
F32, BF16 = jnp.float32, jnp.bfloat16
PLANE_STRIDE = 27
CUBE_STRIDE = 23


def iota(shape, dim):
    return lax.broadcasted_iota(jnp.int32, shape, dim).astype(F32)


def dot(a, b):
    return jnp.dot(a, b, preferred_element_type=F32)


def rem(a, b):
    return lax.rem(a, jnp.int32(b))


def div(a, b):
    return lax.div(a, jnp.int32(b))


def mask(hit):
    return jnp.where(hit, 1.0, 0.0).astype(BF16)


def body(
    sigma_hbm, area_hbm, owner_hbm, slot_hbm, band_hbm, seam, put_in,
    sigma, area, owner, slot, band, loaded, sum1, sum2, filtered, weight, flat, source, source_row, target_row,
    ask_out, ask_in, rep_out, rep_in, put_out, halo_in,
    halo_send, halo_recv, ask_send, ask_recv, rep_send, rep_recv, put_send, put_recv, planes,
):
    orbit, scene, shard = (lax.axis_index(name) for name in ("orbit", "scene", "shard"))
    y, x = div(scene, 4), rem(scene, 4)
    block = scene * 4 + shard

    def plane(k, sign):
        step = rem(k * PLANE_STRIDE, OWNERS)
        dy, dx = sign * div(step, 8) + 4, sign * rem(div(step, 2), 4) + 4
        return (rem(orbit + rem(step, 2), 2), rem(y + dy, 4) * 4 + rem(x + dx, 4), shard)

    def cube(k, sign):
        step = rem(k * CUBE_STRIDE, TRAINERS)
        dy, dx, dz = (sign * d + 4 for d in (div(step, 16), rem(div(step, 4), 4), rem(step, 4)))
        return (orbit, rem(y + dy, 4) * 4 + rem(x + dx, 4), rem(shard + dz, 4))

    def owner_of(device):
        return device[0] * 16 + device[1]

    def trainer_of(device):
        return device[1] * 4 + device[2]

    barrier = pltpu.get_barrier_semaphore()

    def greet(device):
        pl.semaphore_signal(barrier, inc=1, device_id=device, device_id_type=MESH)

    orbits = [rem(orbit + d, 2) for d in range(2)]
    rows_of = [rem(y + d, 4) * 4 for d in range(4)]
    columns_of = [rem(x + d, 4) for d in range(4)]

    def at(offset):
        return (orbits[offset % 2], rows_of[offset // 8] + columns_of[offset // 2 % 4], shard)

    def hops(offset):
        return -sum(min(d, 4 - d) for d in (offset // 8, offset // 2 % 4))

    for offset in sorted(range(1, OWNERS), key=hops):
        greet(at(offset))
    column = [(orbit, scene, rem(shard + d, 4)) for d in range(1, 4)]
    for device in column:
        greet(device)
    for side in (1, TRAINERS - 1):
        peer = rem(block + side, TRAINERS)
        greet((orbit, div(peer, 4), rem(peer, 4)))

    loads = [
        pltpu.make_async_copy(*ends, loaded.at[index])
        for index, ends in enumerate(
            ((owner_hbm, owner), (slot_hbm, slot), (band_hbm, band), (sigma_hbm, sigma), (area_hbm, area))
        )
    ]
    for load in loads:
        load.start()

    for load in loads[:3]:
        load.wait()

    upper = mask(iota((256, 256), 0) < iota((256, 256), 1))
    seen = jnp.zeros((OWNERS + TRAINERS, 1), F32)
    wanted = jnp.zeros((2 * OWNERS, CAPT), F32)
    for part in range(ROWS // 256):
        lanes = pl.ds(part * 256, 256)
        own = owner[:, lanes].astype(F32)
        trainer = ((band[:, lanes] + seam[...]) & (TRAINERS - 1)).astype(F32)
        own_hot = jnp.where(iota((OWNERS, 256), 0) == own, 1.0, 0.0)
        trainer_hot = jnp.where(iota((TRAINERS, 256), 0) == trainer, 1.0, 0.0)
        hot = jnp.concatenate([own_hot, trainer_hot], axis=0)
        before = (dot(hot.astype(BF16), upper) + seen) * hot
        seen = seen + jnp.sum(hot, axis=1, keepdims=True)
        order_in = jnp.sum(before[:OWNERS], axis=0, keepdims=True)
        order_out = jnp.sum(before[OWNERS:], axis=0, keepdims=True)
        source_row[:, lanes] = own * CAPT + order_in
        target_row[:, lanes] = trainer * CAPR + order_out
        place = slot[:, lanes]
        high, low = (place >> 8).astype(F32), (place & 255).astype(F32)
        parts = jnp.concatenate([own_hot * high, own_hot * low], axis=0).astype(BF16)
        wanted = wanted + lax.dot_general(
            parts, mask(iota((CAPT, 256), 0) == order_in),
            (((1,), (1,)), ((), ())), preferred_element_type=F32,
        )
    positions = (wanted[:OWNERS] * 256.0 + wanted[OWNERS:]).astype(jnp.int32)
    for index in range(OWNERS):
        ask_out[index] = positions[index : index + 1, :]

    pl.semaphore_wait(barrier, OWNERS - 1 + 3 + 2)

    pltpu.make_async_copy(ask_out.at[owner_of((orbit, scene))], ask_in.at[0], ask_recv.at[0]).start()

    def send_ask(k, carry):
        peer = plane(k, 1)
        pltpu.make_async_remote_copy(
            ask_out.at[owner_of(peer)], ask_in.at[k], ask_send, ask_recv.at[div(k, RG)],
            device_id=peer, device_id_type=MESH,
        ).start()
        return carry

    lax.fori_loop(1, OWNERS, send_ask, 0)

    def halo_copy(side):
        peer = block + 1 - 2 * side
        rows = pl.ds((1 - side) * (ROWS - HALO), HALO)
        return pltpu.make_async_remote_copy(
            sigma.at[rows], halo_in.at[side], halo_send.at[side], halo_recv.at[side],
            device_id=(orbit, div(peer, 4), rem(peer, 4)), device_id_type=MESH,
        )

    loads[3].wait()
    has_side = (block > 0, block < TRAINERS - 1)
    for side in range(2):

        @pl.when(has_side[1 - side])
        def _():
            halo_copy(side).start()

        @pl.when(jnp.logical_not(has_side[side]))
        def _():
            halo_in[side] = jnp.zeros((HALO, PIX), BF16)

    near = mask(jnp.abs(iota((PIX, PIX), 0) - iota((PIX, PIX), 1)) < 4.0)

    def row_sums(cells, rows):
        wide = cells.astype(F32)
        square = wide * wide
        high = square.astype(BF16)
        low = (square - high.astype(F32)).astype(BF16)
        sum1[rows] = dot(cells, near)
        sum2[rows] = dot(high, near) + dot(low, near)

    def sums_step(part, carry):
        row_sums(sigma[pl.ds(pl.multiple_of(part * 256, 256), 256)], pl.ds(pl.multiple_of(part * 256 + HALO, HALO), 256))
        return carry

    lax.fori_loop(0, ROWS // 256, sums_step, 0)

    loads[4].wait()

    def reply(half, k):
        step = div(k, PG[half])

        @pl.when(k == 0)
        def _():
            pltpu.make_async_copy(rep_out.at[half, k], rep_in.at[half, k], rep_recv.at[half, step]).start()

        @pl.when(k > 0)
        def _():
            pltpu.make_async_remote_copy(
                rep_out.at[half, k], rep_in.at[half, k], rep_send.at[half], rep_recv.at[half, step],
                device_id=plane(k, -1), device_id_type=MESH,
            ).start()

    def gather_step(step, carry):
        group = pl.ds(step * RG, RG)
        pltpu.make_async_copy(ask_in.at[group], ask_in.at[group], ask_recv.at[step]).wait()
        columns = [
            jnp.transpose(jnp.broadcast_to(ask_in[step * RG + j].astype(F32), (CAPT, CAPT)))
            for j in range(RG)
        ]
        column = jnp.concatenate(columns, axis=0)
        lane = iota((RG * CAPT, 128), 1)
        picker = jnp.concatenate([mask(column == lane + 128.0 * c) for c in range(ROWS // 128)], axis=1)
        picked = dot(picker, area[...]).astype(BF16)
        for half in range(2):
            rep_out[half, group] = picked[:, half * HALF : (half + 1) * HALF].reshape(RG, CAPT, HALF)
        for j in range(RG):
            reply(0, step * RG + j)
        return carry

    lax.fori_loop(0, OWNERS // RG, gather_step, 0)

    def reply_rest(k, carry):
        reply(1, k)
        return carry

    lax.fori_loop(0, OWNERS, reply_rest, 0)

    for device in column:
        pl.semaphore_signal(planes, inc=1, device_id=device, device_id_type=MESH)

    for side in range(2):

        @pl.when(has_side[side])
        def _():
            halo_copy(side).wait_recv()

        row_sums(halo_in[side], pl.ds(side * (ROWS + HALO), HALO))

    pixel = iota((LEE, PIX), 1)
    col_span = jnp.minimum(pixel + 3.0, PIX - 1.0) - jnp.maximum(pixel - 3.0, 0.0) + 1.0
    line = iota((LEE, PIX), 0)

    def seven(cells):
        rows = cells.shape[0]
        two = cells + pltpu.roll(cells, rows - 1, 0)
        four = two + pltpu.roll(two, rows - 2, 0)
        total = four + pltpu.roll(two, rows - 4, 0) + pltpu.roll(cells, rows - 6, 0)
        return pltpu.roll(total, rows - 5, 0)[:LEE]

    def lee_step(part, carry):
        start = pl.multiple_of(part * LEE, LEE)
        slab = pl.ds(pl.multiple_of(start + 8, 8), LEE + 16)
        at = line + (block * ROWS + start).astype(F32)
        row_span = jnp.minimum(at + 3.0, TRAINERS * ROWS - 1.0) - jnp.maximum(at - 3.0, 0.0) + 1.0
        share = 1.0 / (row_span * col_span)
        center = sigma[pl.ds(start, LEE)].astype(F32)
        mean = seven(sum1[slab]) * share
        power = mean * mean
        variance = seven(sum2[slab]) * share - power
        speckle = NOISE * power
        mixing = jnp.maximum(variance - speckle, 0.0) / (variance + speckle)
        filtered[pl.ds(start, LEE)] = mean + mixing * (center - mean)
        return carry

    lax.fori_loop(0, ROWS // LEE, lee_step, 0)

    for part in range(ROWS // 128):
        row = source_row[:, pl.ds(part * 128, 128)]
        source[pl.ds(part * 128, 128)] = jnp.transpose(jnp.broadcast_to(row, (128, 128)))


    def pick_step(half, step, carry):
        group = pl.ds(step * PG[half], PG[half])
        landed = rep_in.at[half, group]
        pltpu.make_async_copy(landed, landed, rep_recv.at[half, step]).wait()
        table = rep_in[half, group].reshape(PG[half] * CAPT, HALF)
        firsts = [(owner_of(plane(step * PG[half] + j, 1)) * CAPT).astype(F32) for j in range(PG[half])]
        lane = iota((ROWS, CAPT), 1)
        column = source[...]
        picker = jnp.concatenate([mask(column == lane + first) for first in firsts], axis=1)
        weight[...] = weight[...] + dot(picker, table)
        return carry

    def place_step(half, step, carry):
        group = pl.ds(step * TG[half], TG[half])
        row = target_row[...]
        line = iota((CAPR, ROWS), 0)
        pickers = []
        for j in range(TG[half]):
            first = (trainer_of(cube(step * TG[half] + j, 1)) * CAPR).astype(F32)
            pickers.append(mask(line == row - first))
        placed = dot(jnp.concatenate(pickers, axis=0), flat[...])
        put_out[half, group] = placed.astype(BF16).reshape(TG[half], CAPR, HALF)
        for j in range(TG[half]):
            k = step * TG[half] + j

            @pl.when(k == 0)
            def _():
                pltpu.make_async_copy(put_out.at[half, k], put_in.at[half, block], put_recv.at[half]).start()

            @pl.when(k > 0)
            def _():
                pltpu.make_async_remote_copy(
                    put_out.at[half, k], put_in.at[half, block], put_send.at[half], put_recv.at[half],
                    device_id=cube(k, 1), device_id_type=MESH,
                ).start()

        return carry

    for half in range(2):
        weight[...] = jnp.zeros((ROWS, HALF), F32)
        lax.fori_loop(0, OWNERS // PG[half], functools.partial(pick_step, half), 0)
        if half == 0:
            pl.semaphore_wait(planes, 3)
        flat[...] = (filtered[:, half * HALF : (half + 1) * HALF] * weight[...]).astype(BF16)
        lax.fori_loop(0, TRAINERS // TG[half], functools.partial(place_step, half), 0)

    for half in range(2):
        pltpu.make_async_copy(put_in.at[half], put_in.at[half], put_recv.at[half]).wait()

    sent = [(ask_out.at[pl.ds(1, OWNERS - 1)], ask_send)]
    for half in range(2):
        sent.append((rep_out.at[half, pl.ds(1, OWNERS - 1)], rep_send.at[half]))
        sent.append((put_out.at[half, pl.ds(1, TRAINERS - 1)], put_send.at[half]))
    for part, sem in sent:
        pltpu.make_async_copy(part, part, sem).wait()
    for side in range(2):

        @pl.when(has_side[1 - side])
        def _():
            halo_copy(side).wait_send()


def log_body(values, patches, logs, sems):
    copies = []
    for step in range(TRAINERS // LOG):
        rows = pl.ds(step * LOG * CAPR, LOG * CAPR)
        for half in range(2):
            value = values[half, pl.ds(step * LOG, LOG)].reshape(LOG * CAPR, HALF).astype(F32)
            logs[rows, half * HALF : (half + 1) * HALF] = jnp.where(value > 0.0, jnp.log(value), 0.0)
        copies.append(pltpu.make_async_copy(logs.at[rows], patches.at[rows], sems.at[step]))
        copies[-1].start()
    for copy in copies:
        copy.wait()


def per_device(sigma0, area_tiles, tile_owner, tile_slot, trainer_band, seam_offset):
    vmem = pl.BlockSpec(memory_space=pltpu.VMEM)
    dma = pltpu.SemaphoreType.DMA
    hbm = pl.BlockSpec(memory_space=pltpu.HBM)
    arrived = pl.pallas_call(
        body,
        out_shape=jax.ShapeDtypeStruct((2, TRAINERS, CAPR, HALF), BF16),
        in_specs=[hbm] * 5 + [vmem],
        out_specs=vmem,
        scratch_shapes=[
            pltpu.VMEM((ROWS, PIX), BF16),
            pltpu.VMEM((ROWS, PIX), BF16),
            pltpu.VMEM((1, ROWS), jnp.int32),
            pltpu.VMEM((1, ROWS), jnp.int32),
            pltpu.VMEM((1, ROWS), jnp.int32),
            dma((5,)),
            pltpu.VMEM((ROWS + 2 * HALO, PIX), F32),
            pltpu.VMEM((ROWS + 2 * HALO, PIX), F32),
            pltpu.VMEM((ROWS, PIX), F32),
            pltpu.VMEM((ROWS, HALF), F32),
            pltpu.VMEM((ROWS, HALF), BF16),
            pltpu.VMEM((ROWS, 128), F32),
            pltpu.VMEM((1, ROWS), F32),
            pltpu.VMEM((1, ROWS), F32),
            pltpu.VMEM((OWNERS, 1, CAPT), jnp.int32),
            pltpu.VMEM((OWNERS, 1, CAPT), jnp.int32),
            pltpu.VMEM((2, OWNERS, CAPT, HALF), BF16),
            pltpu.VMEM((2, OWNERS, CAPT, HALF), BF16),
            pltpu.VMEM((2, TRAINERS, CAPR, HALF), BF16),
            pltpu.VMEM((2, HALO, PIX), BF16),
            dma((2,)),
            dma((2,)),
            dma(()),
            dma((OWNERS // RG,)),
            dma((2,)),
            dma((2, OWNERS // min(PG))),
            dma((2,)),
            dma((2,)),
            pltpu.SemaphoreType.REGULAR,
        ],
        compiler_params=pltpu.CompilerParams(
            collective_id=0, has_side_effects=True, vmem_limit_bytes=36 << 20
        ),
        cost_estimate=pl.CostEstimate(flops=16 << 30, bytes_accessed=8 << 20, transcendentals=1 << 20),
    )(
        *(
            pltpu.with_memory_space_constraint(array, pltpu.HBM)
            for array in (
                sigma0[0],
                area_tiles,
                tile_owner.reshape(1, ROWS),
                tile_slot,
                trainer_band.reshape(1, ROWS),
            )
        ),
        seam_offset,
    )
    patches = pl.pallas_call(
        log_body,
        out_shape=jax.ShapeDtypeStruct((TRAINERS * CAPR, PIX), F32),
        in_specs=[vmem],
        out_specs=hbm,
        scratch_shapes=[pltpu.VMEM((TRAINERS * CAPR, PIX), F32), dma((TRAINERS // LOG,))],
        compiler_params=pltpu.CompilerParams(vmem_limit_bytes=16 << 20),
    )(arrived)
    return patches[None]


def solution(mesh):
    return jax.shard_map(
        per_device,
        mesh=mesh,
        in_specs=(
            P("orbit", ("scene", "shard"), None),
            P(("orbit", "scene"), None),
            P("orbit", ("scene", "shard"), None),
            P("orbit", ("scene", "shard")),
            P("orbit", ("scene", "shard"), None),
            P("orbit", ("scene", "shard")),
        ),
        out_specs=P("orbit", ("scene", "shard"), None),
        check_vma=False,
    )
```

```python
import functools

import jax
import jax.numpy as jnp
from jax import lax
from jax.experimental import pallas as pl
from jax.experimental.pallas import tpu as pltpu
from jax.sharding import PartitionSpec as P

NOISE = 0.25
ROWS = 2048
PIX = 256
OWNERS = 32
CAPT = 128
TRAINERS = 64
CAPR = 64
RG = 2
PG = (8, 4)
TG = (32, 4)
LOG = 4
HALO = 16
HALF = PIX // 2
LEE = 64
MESH = pl.DeviceIdType.MESH
F32, BF16 = jnp.float32, jnp.bfloat16
PLANE_STRIDE = 27
CUBE_STRIDE = 23


def iota(shape, dim):
    return lax.broadcasted_iota(jnp.int32, shape, dim).astype(F32)


def dot(a, b):
    return jnp.dot(a, b, preferred_element_type=F32)


def rem(a, b):
    return lax.rem(a, jnp.int32(b))


def div(a, b):
    return lax.div(a, jnp.int32(b))


def mask(hit):
    return jnp.where(hit, 1.0, 0.0).astype(BF16)


def body(
    sigma_hbm, area_hbm, owner_hbm, slot_hbm, band_hbm, seam, put_in,
    sigma, area, owner, slot, band, loaded, sum1, sum2, filtered, weight, flat, source, source_row, target_row,
    ask_out, ask_in, rep_out, rep_in, put_out, halo_in,
    halo_send, halo_recv, ask_send, ask_recv, rep_send, rep_recv, put_send, put_recv, planes,
):
    orbit, scene, shard = (lax.axis_index(name) for name in ("orbit", "scene", "shard"))
    y, x = div(scene, 4), rem(scene, 4)
    block = scene * 4 + shard

    def plane(k, sign):
        step = rem(k * PLANE_STRIDE, OWNERS)
        dy, dx = sign * div(step, 8) + 4, sign * rem(div(step, 2), 4) + 4
        return (rem(orbit + rem(step, 2), 2), rem(y + dy, 4) * 4 + rem(x + dx, 4), shard)

    def cube(k, sign):
        step = rem(k * CUBE_STRIDE, TRAINERS)
        dy, dx, dz = (sign * d + 4 for d in (div(step, 16), rem(div(step, 4), 4), rem(step, 4)))
        return (orbit, rem(y + dy, 4) * 4 + rem(x + dx, 4), rem(shard + dz, 4))

    def owner_of(device):
        return device[0] * 16 + device[1]

    def trainer_of(device):
        return device[1] * 4 + device[2]

    barrier = pltpu.get_barrier_semaphore()

    def greet(device):
        pl.semaphore_signal(barrier, inc=1, device_id=device, device_id_type=MESH)

    orbits = [rem(orbit + d, 2) for d in range(2)]
    rows_of = [rem(y + d, 4) * 4 for d in range(4)]
    columns_of = [rem(x + d, 4) for d in range(4)]

    def at(offset):
        return (orbits[offset % 2], rows_of[offset // 8] + columns_of[offset // 2 % 4], shard)

    def hops(offset):
        return -sum(min(d, 4 - d) for d in (offset // 8, offset // 2 % 4))

    for offset in sorted(range(1, OWNERS), key=hops):
        greet(at(offset))
    column = [(orbit, scene, rem(shard + d, 4)) for d in range(1, 4)]
    for device in column:
        greet(device)
    for side in (1, TRAINERS - 1):
        peer = rem(block + side, TRAINERS)
        greet((orbit, div(peer, 4), rem(peer, 4)))

    loads = [
        pltpu.make_async_copy(*ends, loaded.at[index])
        for index, ends in enumerate(
            ((owner_hbm, owner), (slot_hbm, slot), (band_hbm, band), (sigma_hbm, sigma), (area_hbm, area))
        )
    ]
    for load in loads:
        load.start()

    for load in loads[:3]:
        load.wait()

    upper = mask(iota((256, 256), 0) < iota((256, 256), 1))
    seen = jnp.zeros((OWNERS + TRAINERS, 1), F32)
    wanted = jnp.zeros((2 * OWNERS, CAPT), F32)
    for part in range(ROWS // 256):
        lanes = pl.ds(part * 256, 256)
        own = owner[:, lanes].astype(F32)
        trainer = ((band[:, lanes] + seam[...]) & (TRAINERS - 1)).astype(F32)
        own_hot = jnp.where(iota((OWNERS, 256), 0) == own, 1.0, 0.0)
        trainer_hot = jnp.where(iota((TRAINERS, 256), 0) == trainer, 1.0, 0.0)
        hot = jnp.concatenate([own_hot, trainer_hot], axis=0)
        before = (dot(hot.astype(BF16), upper) + seen) * hot
        seen = seen + jnp.sum(hot, axis=1, keepdims=True)
        order_in = jnp.sum(before[:OWNERS], axis=0, keepdims=True)
        order_out = jnp.sum(before[OWNERS:], axis=0, keepdims=True)
        source_row[:, lanes] = own * CAPT + order_in
        target_row[:, lanes] = trainer * CAPR + order_out
        place = slot[:, lanes]
        high, low = (place >> 8).astype(F32), (place & 255).astype(F32)
        parts = jnp.concatenate([own_hot * high, own_hot * low], axis=0).astype(BF16)
        wanted = wanted + lax.dot_general(
            parts, mask(iota((CAPT, 256), 0) == order_in),
            (((1,), (1,)), ((), ())), preferred_element_type=F32,
        )
    positions = (wanted[:OWNERS] * 256.0 + wanted[OWNERS:]).astype(jnp.int32)
    for index in range(OWNERS):
        ask_out[index] = positions[index : index + 1, :]

    pl.semaphore_wait(barrier, OWNERS - 1 + 3 + 2)

    pltpu.make_async_copy(ask_out.at[owner_of((orbit, scene))], ask_in.at[0], ask_recv.at[0]).start()

    def send_ask(k, carry):
        peer = plane(k, 1)
        pltpu.make_async_remote_copy(
            ask_out.at[owner_of(peer)], ask_in.at[k], ask_send, ask_recv.at[div(k, RG)],
            device_id=peer, device_id_type=MESH,
        ).start()
        return carry

    lax.fori_loop(1, OWNERS, send_ask, 0)

    def halo_copy(side):
        peer = block + 1 - 2 * side
        rows = pl.ds((1 - side) * (ROWS - HALO), HALO)
        return pltpu.make_async_remote_copy(
            sigma.at[rows], halo_in.at[side], halo_send.at[side], halo_recv.at[side],
            device_id=(orbit, div(peer, 4), rem(peer, 4)), device_id_type=MESH,
        )

    loads[3].wait()
    has_side = (block > 0, block < TRAINERS - 1)
    for side in range(2):

        @pl.when(has_side[1 - side])
        def _():
            halo_copy(side).start()

        @pl.when(jnp.logical_not(has_side[side]))
        def _():
            halo_in[side] = jnp.zeros((HALO, PIX), BF16)

    near = mask(jnp.abs(iota((PIX, PIX), 0) - iota((PIX, PIX), 1)) < 4.0)

    def row_sums(cells, rows):
        wide = cells.astype(F32)
        square = wide * wide
        high = square.astype(BF16)
        low = (square - high.astype(F32)).astype(BF16)
        sum1[rows] = dot(cells, near)
        sum2[rows] = dot(high, near) + dot(low, near)

    def sums_step(part, carry):
        row_sums(sigma[pl.ds(pl.multiple_of(part * 256, 256), 256)], pl.ds(pl.multiple_of(part * 256 + HALO, HALO), 256))
        return carry

    lax.fori_loop(0, ROWS // 256, sums_step, 0)

    loads[4].wait()

    def reply(half, k):
        step = div(k, PG[half])

        @pl.when(k == 0)
        def _():
            pltpu.make_async_copy(rep_out.at[half, k], rep_in.at[half, k], rep_recv.at[half, step]).start()

        @pl.when(k > 0)
        def _():
            pltpu.make_async_remote_copy(
                rep_out.at[half, k], rep_in.at[half, k], rep_send.at[half], rep_recv.at[half, step],
                device_id=plane(k, -1), device_id_type=MESH,
            ).start()

    def gather_step(step, carry):
        group = pl.ds(step * RG, RG)
        pltpu.make_async_copy(ask_in.at[group], ask_in.at[group], ask_recv.at[step]).wait()
        columns = [
            jnp.transpose(jnp.broadcast_to(ask_in[step * RG + j].astype(F32), (CAPT, CAPT)))
            for j in range(RG)
        ]
        column = jnp.concatenate(columns, axis=0)
        lane = iota((RG * CAPT, 128), 1)
        picker = jnp.concatenate([mask(column == lane + 128.0 * c) for c in range(ROWS // 128)], axis=1)
        picked = dot(picker, area[...]).astype(BF16)
        for half in range(2):
            rep_out[half, group] = picked[:, half * HALF : (half + 1) * HALF].reshape(RG, CAPT, HALF)
        for j in range(RG):
            reply(0, step * RG + j)
        return carry

    lax.fori_loop(0, OWNERS // RG, gather_step, 0)

    def reply_rest(k, carry):
        reply(1, k)
        return carry

    lax.fori_loop(0, OWNERS, reply_rest, 0)

    for device in column:
        pl.semaphore_signal(planes, inc=1, device_id=device, device_id_type=MESH)

    for side in range(2):

        @pl.when(has_side[side])
        def _():
            halo_copy(side).wait_recv()

        row_sums(halo_in[side], pl.ds(side * (ROWS + HALO), HALO))

    pixel = iota((LEE, PIX), 1)
    col_span = jnp.minimum(pixel + 3.0, PIX - 1.0) - jnp.maximum(pixel - 3.0, 0.0) + 1.0
    line = iota((LEE, PIX), 0)

    def seven(cells):
        rows = cells.shape[0]
        two = cells + pltpu.roll(cells, rows - 1, 0)
        four = two + pltpu.roll(two, rows - 2, 0)
        total = four + pltpu.roll(two, rows - 4, 0) + pltpu.roll(cells, rows - 6, 0)
        return pltpu.roll(total, rows - 5, 0)[:LEE]

    def lee_step(part, carry):
        start = pl.multiple_of(part * LEE, LEE)
        slab = pl.ds(pl.multiple_of(start + 8, 8), LEE + 16)
        at = line + (block * ROWS + start).astype(F32)
        row_span = jnp.minimum(at + 3.0, TRAINERS * ROWS - 1.0) - jnp.maximum(at - 3.0, 0.0) + 1.0
        share = 1.0 / (row_span * col_span)
        center = sigma[pl.ds(start, LEE)].astype(F32)
        mean = seven(sum1[slab]) * share
        power = mean * mean
        variance = seven(sum2[slab]) * share - power
        speckle = NOISE * power
        mixing = jnp.maximum(variance - speckle, 0.0) / (variance + speckle)
        filtered[pl.ds(start, LEE)] = mean + mixing * (center - mean)
        return carry

    lax.fori_loop(0, ROWS // LEE, lee_step, 0)

    for part in range(ROWS // 128):
        row = source_row[:, pl.ds(part * 128, 128)]
        source[pl.ds(part * 128, 128)] = jnp.transpose(jnp.broadcast_to(row, (128, 128)))


    def pick_step(half, step, carry):
        group = pl.ds(step * PG[half], PG[half])
        landed = rep_in.at[half, group]
        pltpu.make_async_copy(landed, landed, rep_recv.at[half, step]).wait()
        table = rep_in[half, group].reshape(PG[half] * CAPT, HALF)
        firsts = [(owner_of(plane(step * PG[half] + j, 1)) * CAPT).astype(F32) for j in range(PG[half])]
        lane = iota((ROWS, CAPT), 1)
        column = source[...]
        picker = jnp.concatenate([mask(column == lane + first) for first in firsts], axis=1)
        weight[...] = weight[...] + dot(picker, table)
        return carry

    def place_step(half, step, carry):
        group = pl.ds(step * TG[half], TG[half])
        row = target_row[...]
        line = iota((CAPR, ROWS), 0)
        pickers = []
        for j in range(TG[half]):
            first = (trainer_of(cube(step * TG[half] + j, 1)) * CAPR).astype(F32)
            pickers.append(mask(line == row - first))
        placed = dot(jnp.concatenate(pickers, axis=0), flat[...])
        put_out[half, group] = placed.astype(BF16).reshape(TG[half], CAPR, HALF)
        for j in range(TG[half]):
            k = step * TG[half] + j

            @pl.when(k == 0)
            def _():
                pltpu.make_async_copy(put_out.at[half, k], put_in.at[half, block], put_recv.at[half]).start()

            @pl.when(k > 0)
            def _():
                pltpu.make_async_remote_copy(
                    put_out.at[half, k], put_in.at[half, block], put_send.at[half], put_recv.at[half],
                    device_id=cube(k, 1), device_id_type=MESH,
                ).start()

        return carry

    for half in range(2):
        weight[...] = jnp.zeros((ROWS, HALF), F32)
        lax.fori_loop(0, OWNERS // PG[half], functools.partial(pick_step, half), 0)
        if half == 0:
            pl.semaphore_wait(planes, 3)
        flat[...] = (filtered[:, half * HALF : (half + 1) * HALF] * weight[...]).astype(BF16)
        lax.fori_loop(0, TRAINERS // TG[half], functools.partial(place_step, half), 0)

    for half in range(2):
        pltpu.make_async_copy(put_in.at[half], put_in.at[half], put_recv.at[half]).wait()

    sent = [(ask_out.at[pl.ds(1, OWNERS - 1)], ask_send)]
    for half in range(2):
        sent.append((rep_out.at[half, pl.ds(1, OWNERS - 1)], rep_send.at[half]))
        sent.append((put_out.at[half, pl.ds(1, TRAINERS - 1)], put_send.at[half]))
    for part, sem in sent:
        pltpu.make_async_copy(part, part, sem).wait()
    for side in range(2):

        @pl.when(has_side[1 - side])
        def _():
            halo_copy(side).wait_send()


def log_body(values, patches, logs, sems):
    copies = []
    for step in range(TRAINERS // LOG):
        rows = pl.ds(step * LOG * CAPR, LOG * CAPR)
        for half in range(2):
            value = values[half, pl.ds(step * LOG, LOG)].reshape(LOG * CAPR, HALF).astype(F32)
            logs[rows, half * HALF : (half + 1) * HALF] = jnp.where(value > 0.0, jnp.log(value), 0.0)
        copies.append(pltpu.make_async_copy(logs.at[rows], patches.at[rows], sems.at[step]))
        copies[-1].start()
    for copy in copies:
        copy.wait()


def per_device(sigma0, area_tiles, tile_owner, tile_slot, trainer_band, seam_offset):
    vmem = pl.BlockSpec(memory_space=pltpu.VMEM)
    dma = pltpu.SemaphoreType.DMA
    hbm = pl.BlockSpec(memory_space=pltpu.HBM)
    arrived = pl.pallas_call(
        body,
        out_shape=jax.ShapeDtypeStruct((2, TRAINERS, CAPR, HALF), BF16),
        in_specs=[hbm] * 5 + [vmem],
        out_specs=vmem,
        scratch_shapes=[
            pltpu.VMEM((ROWS, PIX), BF16),
            pltpu.VMEM((ROWS, PIX), BF16),
            pltpu.VMEM((1, ROWS), jnp.int32),
            pltpu.VMEM((1, ROWS), jnp.int32),
            pltpu.VMEM((1, ROWS), jnp.int32),
            dma((5,)),
            pltpu.VMEM((ROWS + 2 * HALO, PIX), F32),
            pltpu.VMEM((ROWS + 2 * HALO, PIX), F32),
            pltpu.VMEM((ROWS, PIX), F32),
            pltpu.VMEM((ROWS, HALF), F32),
            pltpu.VMEM((ROWS, HALF), BF16),
            pltpu.VMEM((ROWS, 128), F32),
            pltpu.VMEM((1, ROWS), F32),
            pltpu.VMEM((1, ROWS), F32),
            pltpu.VMEM((OWNERS, 1, CAPT), jnp.int32),
            pltpu.VMEM((OWNERS, 1, CAPT), jnp.int32),
            pltpu.VMEM((2, OWNERS, CAPT, HALF), BF16),
            pltpu.VMEM((2, OWNERS, CAPT, HALF), BF16),
            pltpu.VMEM((2, TRAINERS, CAPR, HALF), BF16),
            pltpu.VMEM((2, HALO, PIX), BF16),
            dma((2,)),
            dma((2,)),
            dma(()),
            dma((OWNERS // RG,)),
            dma((2,)),
            dma((2, OWNERS // min(PG))),
            dma((2,)),
            dma((2,)),
            pltpu.SemaphoreType.REGULAR,
        ],
        compiler_params=pltpu.CompilerParams(
            collective_id=0, has_side_effects=True, vmem_limit_bytes=36 << 20
        ),
        cost_estimate=pl.CostEstimate(flops=16 << 30, bytes_accessed=8 << 20, transcendentals=1 << 20),
    )(
        *(
            pltpu.with_memory_space_constraint(array, pltpu.HBM)
            for array in (
                sigma0[0],
                area_tiles,
                tile_owner.reshape(1, ROWS),
                tile_slot,
                trainer_band.reshape(1, ROWS),
            )
        ),
        seam_offset,
    )
    patches = pl.pallas_call(
        log_body,
        out_shape=jax.ShapeDtypeStruct((TRAINERS * CAPR, PIX), F32),
        in_specs=[vmem],
        out_specs=hbm,
        scratch_shapes=[pltpu.VMEM((TRAINERS * CAPR, PIX), F32), dma((TRAINERS // LOG,))],
        compiler_params=pltpu.CompilerParams(vmem_limit_bytes=16 << 20),
    )(arrived)
    return patches[None]


def solution(mesh):
    return jax.shard_map(
        per_device,
        mesh=mesh,
        in_specs=(
            P("orbit", ("scene", "shard"), None),
            P(("orbit", "scene"), None),
            P("orbit", ("scene", "shard"), None),
            P("orbit", ("scene", "shard")),
            P("orbit", ("scene", "shard"), None),
            P("orbit", ("scene", "shard")),
        ),
        out_specs=P("orbit", ("scene", "shard"), None),
        check_vma=False,
    )
```
